32 devices in a mesh: blk: 8 (over y, x, core), uly: 4 (over z).
Axes of the slice: x: 2, y: 2, z: 4, core: 2. Of those that a mesh axis runs over, the one named last changes fastest.
Arguments:
- activations: bfloat16 [3072, 4096], P(('blk', 'uly')), may hold values from -64 to 64
- input_norm_gain: float32 [4096], replicated, may hold values from 0.5 to 2
- query_weight: bfloat16 [4096, 4096], P(None, 'uly'), may hold values from -3 to 3
- key_weight: bfloat16 [4096, 1024], P(None, 'uly'), may hold values from -3 to 3
- value_weight: bfloat16 [4096, 1024], P(None, 'uly'), may hold values from -0.09375 to 0.09375
- output_weight: bfloat16 [4096, 4096], P('uly'), may hold values from -1 to 1
- adapter_down_maps: bfloat16 [4096, 384], replicated, may hold values from -0.09375 to 0.09375
- query_up_maps: bfloat16 [128, 4096], P(None, 'uly'), may hold values from -0.375 to 0.375
- key_up_maps: bfloat16 [128, 1024], P(None, 'uly'), may hold values from -0.375 to 0.375
- value_up_maps: bfloat16 [128, 1024], P(None, 'uly'), may hold values from -0.375 to 0.375
- output_down_maps: bfloat16 [4096, 128], P('uly'), may hold values from -0.5 to 0.5
- output_up_maps: bfloat16 [128, 4096], replicated, may hold values from -1.5 to 1.5
- segment_index: int32 [3072], replicated, may hold values from 0 to 3, never falling along the last dimension, each value on 1 to 2304 neighbouring positions
- segment_adapter: int32 [4], replicated, may hold values from 0 to 7
Outputs:
- attn_out: bfloat16 [3072, 4096], P(('blk', 'uly'))
The draws below stay inside these ranges and needn't reach their ends.
Inputs may be any that keep to these rules, and one draw needn't show every extreme that they name: `segment_index`: never falling along the sequence; each of the 4 segments covers 1 to 2304 tokens, and one covers exactly that many. `segment_adapter`: one adapter per segment; segments may share one.
All inputs are finite; a program needn't handle non-finite values.
Results may differ from the reference program's by a relative error of at most 0.019.
The reference program's roundings to bfloat16 on the way count: a program that leaves them out, or rounds other values in their place, can miss the bound.
Values may be sent and summed in bfloat16 or wider, within the bound.
A program may use at most 192 MiB of HBM per device.

```python
import math
import jax
import jax.numpy as jnp
import numpy as np
from jax import lax

MODEL_WIDTH = 4096
QUERY_HEADS = 32
KEY_VALUE_HEADS = 8
HEAD_SIZE = 128
ADAPTER_RANK = 16
ADAPTER_COUNT = 8
SEGS = 4
TOKEN_COUNT = 3072


def base_query(key):
    return jnp.clip(jax.random.normal(key, (MODEL_WIDTH, QUERY_HEADS * HEAD_SIZE), jnp.float32), -6.0, 6.0)


def draw_query_weight(key, part):
    base_output = base_query(key)
    factor = 1.4
    return jnp.clip(base_output * factor / math.sqrt(MODEL_WIDTH), -3.0, 3.0).astype(jnp.bfloat16)


def draw_key_weight(key, part):
    key = jax.random.fold_in(key, 12)
    random_noise = jnp.clip(jax.random.normal(key, (MODEL_WIDTH, KEY_VALUE_HEADS * HEAD_SIZE), jnp.float32), -6.0, 6.0)
    mixed_heads = 1.4 * random_noise
    return jnp.clip(mixed_heads / math.sqrt(MODEL_WIDTH), -3.0, 3.0).astype(jnp.bfloat16)


def draw_activations(key, part):
    key = jax.random.fold_in(key, 13)
    first = jax.random.fold_in(key, 0)
    base_output = jax.random.normal(first, (TOKEN_COUNT, MODEL_WIDTH), jnp.float32)
    values = base_output
    return jnp.clip(values, -64.0, 64.0).astype(jnp.bfloat16)


def set_ends(result, key, least, high):
    dims = result.shape
    place = [jax.random.randint(jax.random.fold_in(key, axis), (), 0, dims[axis]) for axis in range(len(dims))]
    result = result.at[tuple(place)].set(least)
    longest = dims.index(max(dims))
    place[longest] = (place[longest] + 1) % dims[longest]
    return result.at[tuple(place)].set(high)


def block_levels(key, dims, pieces, low, high):
    loudness, own = 1.0, jax.random.fold_in(key, 6)
    for position, parts in pieces:
        heights = jnp.exp(jax.random.uniform(jax.random.fold_in(own, position), (parts,), jnp.float32, low / len(pieces), high / len(pieces)))
        loudness = loudness * jnp.repeat(heights, dims[position] // parts).reshape([-1 if axis == position else 1 for axis in range(len(dims))])
    return loudness


def profile(count, total, reach, slope):
    portions = [(1 << 20) // math.isqrt(grade ** slope) + 1 for grade in range(2, count + 1)]
    spare, given = total - reach - (count - 1), [1] * (count - 1)
    while spare > 0:
        free = [i for i in range(count - 1) if given[i] < reach]
        mass, remaining = sum([portions[i] for i in free]), spare
        for i in free:
            more = min(reach - given[i], max(1, remaining * portions[i] // mass), spare)
            given[i] = given[i] + more
            spare = spare - more
    return np.array([reach] + given)


def uneven(rng, count, total, bound, lean):
    if count == 2:
        one = jax.random.randint(rng, (), max(1, total - bound), min(bound, total - 1) + 1)
        return jnp.stack([one, total - one])
    sizes = jnp.asarray(profile(count, total, bound, lean), jnp.int32)
    couples = (count - 1) // 2
    donor, taker = sizes[1:1 + 2 * couples:2], sizes[2:2 + 2 * couples:2]
    margin = jnp.minimum(donor - 1, bound - taker)
    passed = jax.random.randint(jax.random.fold_in(rng, 1), (couples,), 0, 1 << 20) % (margin + 1)
    sizes = sizes.at[1:1 + 2 * couples:2].set(donor - passed).at[2:2 + 2 * couples:2].set(taker + passed)
    return sizes[jax.random.permutation(jax.random.fold_in(rng, 2), count)]


def noise(rng, shape, spread, most, cuts=(), held_as=jnp.bfloat16):
    gain = block_levels(rng, shape, cuts, -0.22, 0.18) if cuts else 1.0
    entries = jax.random.normal(rng, shape, jnp.float32) * spread * gain
    return jnp.minimum(jnp.maximum(entries, -most), most).astype(held_as)


def setup_inputs(seed: int = 0) -> dict:
    streams_of = jax.random.split(jax.random.key(seed), 15)
    activations = draw_activations(jax.random.fold_in(streams_of[14], 71), 0)
    input_norm_gain = jnp.clip(jnp.exp(jax.random.uniform(streams_of[1], (MODEL_WIDTH,), jnp.float32, math.log(0.5), math.log(2.0))), 0.5, 2.0)
    query_weight = draw_query_weight(jax.random.fold_in(streams_of[14], 71), 0)
    key_weight = draw_key_weight(jax.random.fold_in(streams_of[14], 71), 0)
    value_weight = noise(streams_of[4], (MODEL_WIDTH, KEY_VALUE_HEADS * HEAD_SIZE), MODEL_WIDTH ** -0.5, 0.09375, ((1, 4),))
    output_weight = noise(streams_of[5], (QUERY_HEADS * HEAD_SIZE, MODEL_WIDTH), (HEAD_SIZE // 4) ** -0.5, 1.0, ((0, 4),))
    adapter_down_maps = noise(streams_of[6], (MODEL_WIDTH, 3 * ADAPTER_COUNT * ADAPTER_RANK), MODEL_WIDTH ** -0.5, 0.09375)
    query_up_maps = noise(streams_of[7], (ADAPTER_COUNT * ADAPTER_RANK, QUERY_HEADS * HEAD_SIZE), (16 * ADAPTER_RANK) ** -0.5, 0.375, ((1, 4),))
    key_up_maps = noise(streams_of[8], (ADAPTER_COUNT * ADAPTER_RANK, KEY_VALUE_HEADS * HEAD_SIZE), (16 * ADAPTER_RANK) ** -0.5, 0.375, ((1, 4),))
    value_up_maps = noise(streams_of[9], (ADAPTER_COUNT * ADAPTER_RANK, KEY_VALUE_HEADS * HEAD_SIZE), (16 * ADAPTER_RANK) ** -0.5, 0.375, ((1, 4),))
    output_down_maps = noise(streams_of[10], (QUERY_HEADS * HEAD_SIZE, ADAPTER_COUNT * ADAPTER_RANK), HEAD_SIZE ** -0.5, 0.5, ((0, 4),))
    output_up_maps = noise(streams_of[11], (ADAPTER_COUNT * ADAPTER_RANK, MODEL_WIDTH), ADAPTER_RANK ** -0.5, 1.5)
    segment_index = jnp.searchsorted(jnp.cumsum(uneven(streams_of[12], SEGS, TOKEN_COUNT, TOKEN_COUNT * 3 // 4, 0)), jnp.arange(TOKEN_COUNT), side="right").astype(jnp.int32)
    segment_adapter = set_ends(jax.random.randint(streams_of[13], (SEGS,), 0, ADAPTER_COUNT), jax.random.fold_in(streams_of[13], 1), 0, ADAPTER_COUNT - 1).astype(jnp.int32)
    return dict(activations=activations, input_norm_gain=input_norm_gain, query_weight=query_weight, key_weight=key_weight, value_weight=value_weight, output_weight=output_weight, adapter_down_maps=adapter_down_maps, query_up_maps=query_up_maps, key_up_maps=key_up_maps, value_up_maps=value_up_maps, output_down_maps=output_down_maps, output_up_maps=output_up_maps, segment_index=segment_index, segment_adapter=segment_adapter)


eps_norm = 1e-05
adapter_scale = 2.0

def tenant_rows(seg_rows, segment_adapter):
    match = seg_rows[:, None] == jnp.arange(segment_adapter.shape[0], dtype=jnp.int32)[None, :]
    return lax.optimization_barrier(jnp.sum(jnp.where(match, segment_adapter[None, :], 0), axis=1)).astype(jnp.int32)

def normalize(activations, input_norm_gain):
    values = activations.astype(jnp.float32)
    power = lax.optimization_barrier(jnp.mean(values * values, axis=1, keepdims=True))
    return (values * lax.rsqrt(power + eps_norm) * input_norm_gain[None, :]).astype(jnp.bfloat16)

def tenant_adapter_mask(tenant_index, hidden_width):
    columns = jnp.arange(hidden_width, dtype=jnp.int32) // ADAPTER_RANK % ADAPTER_COUNT
    return columns[None, :] == tenant_index[:, None]

def attend(query_rows, key_matrix_rows, value_matrix_rows, segment_index):
    query_group = QUERY_HEADS // KEY_VALUE_HEADS
    token_block = math.gcd(TOKEN_COUNT, 256)
    score_scale = 1.0 / math.sqrt(HEAD_SIZE)
    positions = jnp.arange(TOKEN_COUNT, dtype=jnp.int32)
    every_key = key_matrix_rows.astype(jnp.float32).reshape(TOKEN_COUNT, KEY_VALUE_HEADS, HEAD_SIZE)
    every_value = value_matrix_rows.astype(jnp.float32).reshape(TOKEN_COUNT, KEY_VALUE_HEADS, HEAD_SIZE)
    query_matrix = query_rows.reshape(TOKEN_COUNT // token_block, token_block, KEY_VALUE_HEADS, query_group, HEAD_SIZE)
    starts = jnp.arange(TOKEN_COUNT // token_block, dtype=jnp.int32) * token_block

    def one_block(input_rows):
        rows_in, start = input_rows
        query_pos = start + jnp.arange(token_block, dtype=jnp.int32)
        query_seg = lax.dynamic_slice_in_dim(segment_index, start, token_block)
        allowed = (positions[None, :] <= query_pos[:, None]) & (segment_index[None, :] == query_seg[:, None])
        allowed = allowed[:, None, None, :]
        scores = jnp.einsum('rkgd,nkd->rkgn', rows_in.astype(jnp.float32), every_key) * score_scale
        peak = lax.optimization_barrier(jnp.max(jnp.where(allowed, scores, -1e+30), axis=3, keepdims=True))
        weights = jnp.where(allowed, jnp.exp(scores - peak), 0.0)
        total = lax.optimization_barrier(jnp.sum(weights, axis=3))
        rounded = lax.optimization_barrier(weights.astype(jnp.bfloat16)).astype(jnp.float32)
        summed = jnp.einsum('rkgn,nkd->rkgd', rounded, every_value)
        return (summed / total[..., None]).reshape(token_block, QUERY_HEADS * HEAD_SIZE).astype(jnp.bfloat16)
    return lax.map(one_block, (query_matrix, starts)).reshape(TOKEN_COUNT, QUERY_HEADS * HEAD_SIZE)

def reference(activations, input_norm_gain, query_weight, key_weight, value_weight, output_weight, adapter_down_maps, query_up_maps, key_up_maps, value_up_maps, output_down_maps, output_up_maps, segment_index, segment_adapter):
    hidden_width = ADAPTER_COUNT * ADAPTER_RANK
    normed_input = normalize(activations, input_norm_gain)
    tenant_index = tenant_rows(segment_index, segment_adapter)
    lowered_rows = jnp.where(tenant_adapter_mask(tenant_index, 3 * hidden_width), jnp.dot(normed_input, adapter_down_maps, preferred_element_type=jnp.float32), 0.0).astype(jnp.bfloat16)
    query_rows = (jnp.dot(normed_input, query_weight, preferred_element_type=jnp.float32) + adapter_scale * jnp.dot(lowered_rows[:, :hidden_width], query_up_maps, preferred_element_type=jnp.float32)).astype(jnp.bfloat16)
    key_matrix_rows = (jnp.dot(normed_input, key_weight, preferred_element_type=jnp.float32) + adapter_scale * jnp.dot(lowered_rows[:, hidden_width:2 * hidden_width], key_up_maps, preferred_element_type=jnp.float32)).astype(jnp.bfloat16)
    value_matrix_rows = (jnp.dot(normed_input, value_weight, preferred_element_type=jnp.float32) + adapter_scale * jnp.dot(lowered_rows[:, 2 * hidden_width:], value_up_maps, preferred_element_type=jnp.float32)).astype(jnp.bfloat16)
    mixed_heads = attend(query_rows, key_matrix_rows, value_matrix_rows, segment_index)
    rank_rows = jnp.where(tenant_adapter_mask(tenant_index, hidden_width), jnp.dot(mixed_heads, output_down_maps, preferred_element_type=jnp.float32), 0.0)
    block_result = jnp.dot(mixed_heads, output_weight, preferred_element_type=jnp.float32) + adapter_scale * jnp.dot(rank_rows, output_up_maps.astype(jnp.float32), precision=lax.Precision.HIGHEST)
    return block_result.astype(jnp.bfloat16)
```

```python
import functools
import math

import jax
import jax.numpy as jnp
from jax import lax
from jax.experimental import pallas as pl
from jax.experimental.pallas import tpu as pltpu
from jax.sharding import PartitionSpec as P

QUERY_HEADS = 32
KEY_VALUE_HEADS = 8
HEAD_SIZE = 128
ADAPTER_RANK = 16
ADAPTER_COUNT = 8
HIDDEN = ADAPTER_COUNT * ADAPTER_RANK

eps_norm = 1e-05
adapter_scale = 2.0
MESH = pl.DeviceIdType.MESH
VMEM_LIMIT = 60 * 1024 * 1024
MASKED = -1e30


def segment_starts(seg_ref, segments):
    seg = seg_ref[...]
    starts = []
    for k in range(segments):
        below = jnp.where(seg < k, 1.0, 0.0)
        starts.append(jnp.sum(jnp.sum(below, axis=1, keepdims=True), axis=0, keepdims=True))
    return starts


def tenant_mask(starts, adapter_ref, first, rows, width):
    pos = (first + lax.broadcasted_iota(jnp.int32, (rows, width), 0)).astype(jnp.float32)
    column = lax.broadcasted_iota(jnp.int32, (rows, width), 1)
    column = (column // ADAPTER_RANK) % ADAPTER_COUNT
    tenant = jnp.zeros((rows, width), jnp.int32) + adapter_ref[0]
    for k in range(1, len(starts)):
        tenant = jnp.where(pos >= starts[k], adapter_ref[k], tenant)
    return column == tenant


def gather_kernel(
    H, B, C, segments,
    x_ref, gain_ref, down_ref, wq_ref, wk_ref, wv_ref, uq_ref, uk_ref, uv_ref, seg_ref, adapter_ref,
    q_ref, kv_ref,
    rows_buf, weights, kv_buf, w_sem, send_sem, recv_sem, kv_send, kv_recv, kv_local,
):
    u = lax.axis_index("uly")
    b = lax.axis_index("blk")
    rows = x_ref.shape[0]
    part = rows // C
    kw = wk_ref.shape[1]
    qw = wq_ref.shape[1]

    def weight_copies():
        return [
            pltpu.make_async_copy(wk_ref, weights.at[:, pl.ds(0, kw)], w_sem.at[0]),
            pltpu.make_async_copy(wv_ref, weights.at[:, pl.ds(kw, kw)], w_sem.at[1]),
            pltpu.make_async_copy(wq_ref, weights.at[:, pl.ds(2 * kw, qw)], w_sem.at[2]),
        ]

    for copy in weight_copies():
        copy.start()

    barrier = pltpu.get_barrier_semaphore()

    @pl.when(u > 0)
    def _():
        pl.semaphore_signal(barrier, inc=1, device_id=(b, u - 1), device_id_type=MESH)

    @pl.when(u < H - 1)
    def _():
        pl.semaphore_signal(barrier, inc=1, device_id=(b, u + 1), device_id_type=MESH)

    for d in range(1, B):
        pl.semaphore_signal(
            barrier, inc=1, device_id=(lax.rem(b + d, B), u), device_id_type=MESH
        )

    def send(j, c, side):
        where = rows_buf.at[j, pl.ds(c * part, part), :]
        return pltpu.make_async_remote_copy(
            src_ref=where,
            dst_ref=where,
            send_sem=send_sem.at[side, j, c],
            recv_sem=recv_sem.at[j, c],
            device_id=(b, u - 1 if side == 0 else u + 1),
            device_id_type=MESH,
        )

    def send_if(j, c):
        @pl.when((j >= u) & (u > 0))
        def _():
            send(j, c, 0).start()

        @pl.when((j <= u) & (u < H - 1))
        def _():
            send(j, c, 1).start()

    def normalize(c):
        values = x_ref[pl.ds(c * part, part), :].astype(jnp.float32)
        power = jnp.mean(values * values, axis=1, keepdims=True)
        normed = values * lax.rsqrt(power + eps_norm) * gain_ref[...]
        rows_buf[u, pl.ds(c * part, part), :] = normed.astype(jnp.bfloat16)

    normalize(0)

    @pl.when((u > 0) & (u < H - 1))
    def _():
        pl.semaphore_wait(barrier, B + 1)

    @pl.when((u == 0) | (u == H - 1))
    def _():
        pl.semaphore_wait(barrier, B)

    send_if(u, 0)
    for c in range(1, C):
        normalize(c)
        send_if(u, c)

    starts = segment_starts(seg_ref, segments)
    for copy in weight_copies():
        copy.wait()

    def kv_copy(j, d):
        return pltpu.make_async_remote_copy(
            src_ref=kv_buf.at[j],
            dst_ref=kv_ref.at[pl.ds(pl.multiple_of((b * H + j) * rows, rows), rows), :],
            send_sem=kv_send.at[d, j],
            recv_sem=kv_recv.at[d, j],
            device_id=(b + d, u),
            device_id_type=MESH,
        )

    def kv_own(j):
        return pltpu.make_async_copy(
            kv_buf.at[j],
            kv_ref.at[pl.ds(pl.multiple_of((b * H + j) * rows, rows), rows), :],
            kv_local.at[j],
        )

    def project(j):
        shard = rows_buf[j]
        mask = tenant_mask(starts, adapter_ref, (b * H + j) * rows, rows, HIDDEN)

        def lowered(which):
            raw = jnp.dot(
                shard,
                down_ref[:, which * HIDDEN : (which + 1) * HIDDEN],
                preferred_element_type=jnp.float32,
            )
            return jnp.where(mask, raw, 0.0).astype(jnp.bfloat16)

        def product(column, width, low, up):
            return (
                jnp.dot(
                    shard, weights[:, pl.ds(column, width)], preferred_element_type=jnp.float32
                )
                + adapter_scale * jnp.dot(low, up, preferred_element_type=jnp.float32)
            ).astype(jnp.bfloat16)

        kv_buf[j, :, :kw] = product(0, kw, lowered(1), uk_ref[...])
        kv_buf[j, :, kw:] = product(kw, kw, lowered(2), uv_ref[...])
        kv_own(j).start()
        for d in range(1, B):
            @pl.when(b + d < B)
            def _():
                kv_copy(j, d).start()

        low = lowered(0)
        step = 256

        def query_tile(n, carry):
            at = pl.multiple_of(n * step, step)
            q_ref[pl.ds(pl.multiple_of(j * rows, rows), rows), pl.ds(at, step)] = product(
                2 * kw + at, step, low, uq_ref[:, pl.ds(at, step)]
            )
            return carry

        lax.fori_loop(0, qw // step, query_tile, 0)

    def phase(d, carry):
        @pl.when(d > 0)
        def _():
            for c in range(C):
                @pl.when(u + d < H)
                def _():
                    send(u + d, c, 0).wait_recv()

                    @pl.when(u > 0)
                    def _():
                        send(u + d, c, 0).start()

                @pl.when(u - d >= 0)
                def _():
                    send(u - d, c, 1).wait_recv()

                    @pl.when(u < H - 1)
                    def _():
                        send(u - d, c, 1).start()

        def side_step(side, inner):
            j = u + d * (1 - 2 * side)

            @pl.when((j >= 0) & (j < H) & (d + 1 > side))
            def _():
                project(j)

            return inner

        lax.fori_loop(0, jnp.where(d > 0, 2, 1), side_step, 0)
        return carry

    lax.fori_loop(0, H, phase, 0)

    def finish(j, carry):
        for c in range(C):
            @pl.when((j >= u) & (u > 0))
            def _():
                send(j, c, 0).wait_send()

            @pl.when((j <= u) & (u < H - 1))
            def _():
                send(j, c, 1).wait_send()

        kv_own(j).wait()
        for d in range(1, B):
            @pl.when(b + d < B)
            def _():
                kv_copy(j, d).wait_send()

            @pl.when(b - d >= 0)
            def _():
                kv_copy(j, d).wait_recv()

        return carry

    lax.fori_loop(0, H, finish, 0)


def attention_kernel(
    tile, groups, segments, q_ref, kv_ref, seg_ref, mixed_ref, bias, peak, total
):
    b = lax.axis_index("blk")
    rows = q_ref.shape[0]
    blocks = rows // tile
    group = QUERY_HEADS // KEY_VALUE_HEADS
    scale = math.log2(math.e) / math.sqrt(HEAD_SIZE)
    starts = segment_starts(seg_ref, segments)

    def query_block(qi, carry):
        own = b * blocks + qi
        at_rows = pl.ds(pl.multiple_of(qi * tile, tile), tile)
        pos = (own * tile + lax.broadcasted_iota(jnp.int32, (tile, 1), 0)).astype(jnp.float32)
        lower = jnp.zeros((tile, 1), jnp.float32)
        for k in range(1, segments):
            lower = jnp.where(pos >= starts[k], starts[k], lower)
        first = jnp.min(lower).astype(jnp.int32) // tile
        peak[...] = jnp.full_like(peak, MASKED)
        total[...] = jnp.zeros_like(total)

        def key_tile(i, inner):
            index = own - i
            at_keys = pl.ds(pl.multiple_of(index * tile, tile), tile)
            key_pos = (index * tile + lax.broadcasted_iota(jnp.int32, (tile, tile), 1)).astype(
                jnp.float32
            )
            bias[...] = jnp.where((key_pos <= pos) & (key_pos >= lower), 0.0, MASKED)
            for g in range(groups):
                keys = kv_ref[at_keys, g * HEAD_SIZE : (g + 1) * HEAD_SIZE]
                values = kv_ref[at_keys, (groups + g) * HEAD_SIZE : (groups + g + 1) * HEAD_SIZE]
                values = jnp.concatenate([values, jnp.ones_like(values)], axis=1)
                for h in range(g * group, (g + 1) * group):
                    query = q_ref[at_rows, h * HEAD_SIZE : (h + 1) * HEAD_SIZE]
                    scores = lax.dot_general(
                        query, keys, (((1,), (1,)), ((), ())), preferred_element_type=jnp.float32
                    )
                    scores = scores * scale + bias[...]
                    before = peak[h]
                    fresh = jnp.maximum(before, jnp.max(scores, axis=1, keepdims=True))
                    weights = jnp.exp2(scores - fresh[:, :1]).astype(jnp.bfloat16)
                    decay = jnp.exp2(before - fresh)
                    peak[h] = fresh
                    total[h] = total[h] * jnp.concatenate([decay, decay], axis=1) + jnp.dot(
                        weights, values, preferred_element_type=jnp.float32
                    )
            return inner

        lax.fori_loop(0, own - first + 1, key_tile, 0)
        for h in range(groups * group):
            mixed_ref[at_rows, h * HEAD_SIZE : (h + 1) * HEAD_SIZE] = (
                total[h, :, :HEAD_SIZE] / total[h, :, HEAD_SIZE:]
            ).astype(jnp.bfloat16)
        return carry

    lax.fori_loop(0, blocks, query_block, 0)


def output_kernel(
    H, C, segments,
    mixed_ref, wo_ref, down_ref, up_ref, seg_ref, adapter_ref,
    out_ref,
    left, weights, sent, landed, w_sem, up_sem, send_sem, recv_sem,
):
    u = lax.axis_index("uly")
    b = lax.axis_index("blk")
    rows = out_ref.shape[0]
    inner = mixed_ref.shape[1]
    width = out_ref.shape[1] // C

    def weight_copy(c):
        columns = pl.ds(pl.multiple_of(c * width, width), width)
        return pltpu.make_async_copy(
            wo_ref.at[:, columns], weights.at[pl.ds(0, inner), columns], w_sem.at[c]
        )

    def up_copy(i):
        return pltpu.make_async_copy(
            up_ref, weights.at[pl.ds(inner + i * HIDDEN, HIDDEN), :], up_sem.at[i]
        )

    up_copy(0).start()
    up_copy(1).start()
    for c in range(C):
        weight_copy(c).start()

    barrier = pltpu.get_barrier_semaphore()

    @pl.when(u > 0)
    def _():
        pl.semaphore_signal(barrier, inc=1, device_id=(b, u - 1), device_id_type=MESH)

    @pl.when(u < H - 1)
    def _():
        pl.semaphore_signal(barrier, inc=1, device_id=(b, u + 1), device_id_type=MESH)

    starts = segment_starts(seg_ref, segments)
    total_rows = H * rows
    lows = jnp.dot(mixed_ref[...], down_ref[...], preferred_element_type=jnp.float32)
    mask = tenant_mask(starts, adapter_ref, b * total_rows, total_rows, HIDDEN)
    lows = jnp.where(mask, adapter_scale * lows, 0.0)
    high = lows.astype(jnp.bfloat16)
    left[:, :inner] = mixed_ref[...]
    left[:, inner : inner + HIDDEN] = high
    left[:, inner + HIDDEN :] = (lows - high.astype(jnp.float32)).astype(jnp.bfloat16)

    @pl.when((u > 0) & (u < H - 1))
    def _():
        pl.semaphore_wait(barrier, 2)

    @pl.when((u == 0) | (u == H - 1))
    def _():
        pl.semaphore_wait(barrier, 1)

    up_copy(0).wait()
    up_copy(1).wait()

    def own_part(j, c):
        at_rows = pl.ds(pl.multiple_of(j * rows, rows), rows)
        columns = pl.ds(pl.multiple_of(c * width, width), width)
        return jnp.dot(left[at_rows, :], weights[:, columns], preferred_element_type=jnp.float32)

    def hop(j, c, side):
        return pltpu.make_async_remote_copy(
            src_ref=sent.at[j, c],
            dst_ref=landed.at[side, j, c],
            send_sem=send_sem.at[j, c],
            recv_sem=recv_sem.at[side, j, c],
            device_id=(b, u + 2 * side - 1),
            device_id_type=MESH,
        )

    def step(p, carry):
        def chunk(c, inner_carry):
            @pl.when(p == 0)
            def _():
                weight_copy(c).wait()

            def pass_on(side, side_carry):
                j = jnp.where(side == 0, p, H - 1 - p)

                @pl.when(jnp.where(side == 0, u - j, j - u) > 0)
                def _():
                    value = own_part(j, c)

                    @pl.when(jnp.where(side == 0, H - 1 - u, u) > 0)
                    def _():
                        hop(j, c, side).wait_recv()
                        sent[j, c] = (value + landed[side, j, c].astype(jnp.float32)).astype(
                            jnp.bfloat16
                        )

                    @pl.when(jnp.where(side == 0, H - 1 - u, u) == 0)
                    def _():
                        sent[j, c] = value.astype(jnp.bfloat16)

                    hop(j, c, side).start()

                return side_carry

            lax.fori_loop(0, 2, pass_on, 0)
            return inner_carry

        lax.fori_loop(0, C, chunk, 0)
        return carry

    lax.fori_loop(0, H - 1, step, 0)

    def last(c, carry):
        columns = pl.ds(pl.multiple_of(c * width, width), width)
        sent_own = own_part(u, c)

        @pl.when(u > 0)
        def _():
            hop(u, c, 1).wait_recv()

        @pl.when(u < H - 1)
        def _():
            hop(u, c, 0).wait_recv()

        from_left = jnp.where(u > 0, landed[1, u, c].astype(jnp.float32), 0.0)
        from_right = jnp.where(u < H - 1, landed[0, u, c].astype(jnp.float32), 0.0)
        out_ref[:, columns] = (sent_own + from_left + from_right).astype(jnp.bfloat16)
        return carry

    lax.fori_loop(0, C, last, 0)

    def finish(j, carry):
        for c in range(C):
            @pl.when(j < u)
            def _():
                hop(j, c, 0).wait_send()

            @pl.when(j > u)
            def _():
                hop(j, c, 1).wait_send()

        return carry

    lax.fori_loop(0, H, finish, 0)


IN_VMEM = pl.BlockSpec(memory_space=pltpu.VMEM)
IN_SMEM = pl.BlockSpec(memory_space=pltpu.SMEM)
ANYWHERE = pl.BlockSpec(memory_space=pl.ANY)


def shards(
    activations,
    input_norm_gain,
    query_weight,
    key_weight,
    value_weight,
    output_weight,
    adapter_down_maps,
    query_up_maps,
    key_up_maps,
    value_up_maps,
    output_down_maps,
    output_up_maps,
    segment_index,
    segment_adapter,
):
    H = lax.axis_size("uly")
    B = lax.axis_size("blk")
    rows, features = activations.shape
    tokens = segment_index.shape[0]
    segments = segment_adapter.shape[0]
    qw = query_weight.shape[1]
    kw = key_weight.shape[1]
    block_rows = rows * H
    seg = segment_index.reshape(tokens // 128, 128)
    bf16 = jnp.bfloat16
    C = 3
    queries, keys_values = pl.pallas_call(
        functools.partial(gather_kernel, H, B, C, segments),
        out_shape=(
            jax.ShapeDtypeStruct((block_rows, qw), bf16),
            jax.ShapeDtypeStruct((tokens, 2 * kw), bf16),
        ),
        in_specs=[IN_VMEM, IN_VMEM, IN_VMEM, ANYWHERE, ANYWHERE, ANYWHERE]
        + [IN_VMEM] * 4
        + [IN_SMEM],
        out_specs=(IN_VMEM, ANYWHERE),
        scratch_shapes=[
            pltpu.VMEM((H, rows, features), bf16),
            pltpu.VMEM((features, qw + 2 * kw), bf16),
            pltpu.VMEM((H, rows, 2 * kw), bf16),
            pltpu.SemaphoreType.DMA((3,)),
            pltpu.SemaphoreType.DMA((2, H, C)),
            pltpu.SemaphoreType.DMA((H, C)),
            pltpu.SemaphoreType.DMA((B, H)),
            pltpu.SemaphoreType.DMA((B, H)),
            pltpu.SemaphoreType.DMA((H,)),
        ],
        compiler_params=pltpu.CompilerParams(
            collective_id=0, has_side_effects=True, vmem_limit_bytes=VMEM_LIMIT
        ),
        name="gather_project",
    )(
        activations,
        input_norm_gain.reshape(1, features),
        adapter_down_maps,
        query_weight,
        key_weight,
        value_weight,
        query_up_maps,
        key_up_maps,
        value_up_maps,
        seg,
        segment_adapter,
    )

    tile = math.gcd(block_rows, 384)
    heads = qw // HEAD_SIZE
    mixed = pl.pallas_call(
        functools.partial(attention_kernel, tile, kw // HEAD_SIZE, segments),
        out_shape=jax.ShapeDtypeStruct((block_rows, qw), bf16),
        in_specs=[IN_VMEM] * 3,
        out_specs=IN_VMEM,
        scratch_shapes=[
            pltpu.VMEM((tile, tile), jnp.float32),
            pltpu.VMEM((heads, tile, HEAD_SIZE), jnp.float32),
            pltpu.VMEM((heads, tile, 2 * HEAD_SIZE), jnp.float32),
        ],
        compiler_params=pltpu.CompilerParams(vmem_limit_bytes=VMEM_LIMIT),
        name="attend",
    )(queries, keys_values, seg)

    C = 4
    return pl.pallas_call(
        functools.partial(output_kernel, H, C, segments),
        out_shape=jax.ShapeDtypeStruct((rows, features), bf16),
        in_specs=[IN_VMEM, ANYWHERE, IN_VMEM, ANYWHERE, IN_VMEM, IN_SMEM],
        out_specs=IN_VMEM,
        scratch_shapes=[
            pltpu.VMEM((block_rows, qw + 2 * HIDDEN), bf16),
            pltpu.VMEM((qw + 2 * HIDDEN, features), bf16),
            pltpu.VMEM((H, C, rows, features // C), bf16),
            pltpu.VMEM((2, H, C, rows, features // C), bf16),
            pltpu.SemaphoreType.DMA((C,)),
            pltpu.SemaphoreType.DMA((2,)),
            pltpu.SemaphoreType.DMA((H, C)),
            pltpu.SemaphoreType.DMA((2, H, C)),
        ],
        compiler_params=pltpu.CompilerParams(
            collective_id=1, has_side_effects=True, vmem_limit_bytes=VMEM_LIMIT
        ),
        name="project_reduce",
    )(mixed, output_weight, output_down_maps, output_up_maps, seg, segment_adapter)


def solution(mesh):
    return jax.shard_map(
        shards,
        mesh=mesh,
        in_specs=(
            P(("blk", "uly"), None),
            P(),
            P(None, "uly"),
            P(None, "uly"),
            P(None, "uly"),
            P("uly", None),
            P(),
            P(None, "uly"),
            P(None, "uly"),
            P(None, "uly"),
            P("uly", None),
            P(),
            P(),
            P(),
        ),
        out_specs=P(("blk", "uly"), None),
        check_vma=False,
    )
```

```python
import functools
import math

import jax
import jax.numpy as jnp
from jax import lax
from jax.experimental import pallas as pl
from jax.experimental.pallas import tpu as pltpu
from jax.sharding import PartitionSpec as P

QUERY_HEADS = 32
KEY_VALUE_HEADS = 8
HEAD_SIZE = 128
ADAPTER_RANK = 16
ADAPTER_COUNT = 8
HIDDEN = ADAPTER_COUNT * ADAPTER_RANK

eps_norm = 1e-05
adapter_scale = 2.0
MESH = pl.DeviceIdType.MESH
VMEM_LIMIT = 60 * 1024 * 1024
MASKED = -1e30


def segment_starts(seg_ref, segments):
    seg = seg_ref[...]
    starts = []
    for k in range(segments):
        below = jnp.where(seg < k, 1.0, 0.0)
        starts.append(jnp.sum(jnp.sum(below, axis=1, keepdims=True), axis=0, keepdims=True))
    return starts


def tenant_mask(starts, adapter_ref, first, rows, width):
    pos = (first + lax.broadcasted_iota(jnp.int32, (rows, width), 0)).astype(jnp.float32)
    column = lax.broadcasted_iota(jnp.int32, (rows, width), 1)
    column = (column // ADAPTER_RANK) % ADAPTER_COUNT
    tenant = jnp.zeros((rows, width), jnp.int32) + adapter_ref[0]
    for k in range(1, len(starts)):
        tenant = jnp.where(pos >= starts[k], adapter_ref[k], tenant)
    return column == tenant


def block_kernel(
    H, B, C, D, T, segments,
    x_ref, gain_ref, down_ref, wq_ref, wk_ref, wv_ref, uq_ref, uk_ref, uv_ref,
    wo_ref, out_down_ref, out_up_ref, seg_ref, adapter_ref,
    out_ref,
    rows_buf, weights, down, q_buf, kv, peak, total, left, out_weights, sent, landed,
    w_sem, o_sem, send_sem, recv_sem, kv_send, kv_recv, hop_send, hop_recv,
):
    u = lax.axis_index("uly")
    b = lax.axis_index("blk")
    rows, features = x_ref.shape
    part = rows // C
    kw = wk_ref.shape[1]
    qw = wq_ref.shape[1]
    width = features // D

    def weight_copies():
        return [
            pltpu.make_async_copy(down_ref, down, w_sem.at[0]),
            pltpu.make_async_copy(wk_ref, weights.at[:, pl.ds(0, kw)], w_sem.at[1]),
            pltpu.make_async_copy(wv_ref, weights.at[:, pl.ds(kw, kw)], w_sem.at[2]),
            pltpu.make_async_copy(wq_ref, weights.at[:, pl.ds(2 * kw, qw)], w_sem.at[3]),
        ]

    def output_copies():
        return [
            pltpu.make_async_copy(wo_ref, out_weights.at[pl.ds(0, qw), :], o_sem.at[0]),
            pltpu.make_async_copy(
                out_up_ref, out_weights.at[pl.ds(qw, HIDDEN), :], o_sem.at[1]
            ),
            pltpu.make_async_copy(
                out_up_ref, out_weights.at[pl.ds(qw + HIDDEN, HIDDEN), :], o_sem.at[2]
            ),
        ]

    for copy in weight_copies():
        copy.start()
    kv[...] = jnp.zeros_like(kv)

    barrier = pltpu.get_barrier_semaphore()

    @pl.when(u > 0)
    def _():
        pl.semaphore_signal(barrier, inc=1, device_id=(b, u - 1), device_id_type=MESH)

    @pl.when(u < H - 1)
    def _():
        pl.semaphore_signal(barrier, inc=1, device_id=(b, u + 1), device_id_type=MESH)

    for d in range(1, B):
        pl.semaphore_signal(
            barrier, inc=1, device_id=(lax.rem(b + d, B), u), device_id_type=MESH
        )

    def send(j, c, side):
        where = rows_buf.at[j, pl.ds(c * part, part), :]
        return pltpu.make_async_remote_copy(
            src_ref=where,
            dst_ref=where,
            send_sem=send_sem.at[side, j, c],
            recv_sem=recv_sem.at[j, c],
            device_id=(b, u - 1 if side == 0 else u + 1),
            device_id_type=MESH,
        )

    def send_if(j, c):
        @pl.when((j >= u) & (u > 0))
        def _():
            send(j, c, 0).start()

        @pl.when((j <= u) & (u < H - 1))
        def _():
            send(j, c, 1).start()

    def normalize(c):
        values = x_ref[pl.ds(c * part, part), :].astype(jnp.float32)
        power = jnp.mean(values * values, axis=1, keepdims=True)
        normed = values * lax.rsqrt(power + eps_norm) * gain_ref[...]
        rows_buf[u, pl.ds(c * part, part), :] = normed.astype(jnp.bfloat16)

    normalize(0)

    @pl.when((u > 0) & (u < H - 1))
    def _():
        pl.semaphore_wait(barrier, B + 1)

    @pl.when((u == 0) | (u == H - 1))
    def _():
        pl.semaphore_wait(barrier, B)

    send_if(u, 0)
    for c in range(1, C):
        normalize(c)
        send_if(u, c)

    starts = segment_starts(seg_ref, segments)
    for copy in weight_copies():
        copy.wait()
    for copy in output_copies():
        copy.start()

    def shard_rows(block, j):
        return pl.ds(pl.multiple_of((block * H + j) * rows, rows), rows)

    def kv_copy(j, d):
        where = kv.at[shard_rows(b, j), :]
        return pltpu.make_async_remote_copy(
            src_ref=where,
            dst_ref=where,
            send_sem=kv_send.at[d, j],
            recv_sem=kv_recv.at[d, j],
            device_id=(b + d, u),
            device_id_type=MESH,
        )

    def project(j):
        shard = rows_buf[j]
        mask = tenant_mask(starts, adapter_ref, (b * H + j) * rows, rows, HIDDEN)

        def lowered(which):
            raw = jnp.dot(
                shard,
                down[:, which * HIDDEN : (which + 1) * HIDDEN],
                preferred_element_type=jnp.float32,
            )
            return jnp.where(mask, raw, 0.0).astype(jnp.bfloat16)

        def product(column, width, low, up):
            return (
                jnp.dot(
                    shard, weights[:, pl.ds(column, width)], preferred_element_type=jnp.float32
                )
                + adapter_scale * jnp.dot(low, up, preferred_element_type=jnp.float32)
            ).astype(jnp.bfloat16)

        kv[shard_rows(b, j), :kw] = product(0, kw, lowered(1), uk_ref[...])
        kv[shard_rows(b, j), kw:] = product(kw, kw, lowered(2), uv_ref[...])
        for d in range(1, B):
            @pl.when(b + d < B)
            def _():
                kv_copy(j, d).start()

        low = lowered(0)
        step = 256

        def query_tile(n, carry):
            at = pl.multiple_of(n * step, step)
            q_buf[shard_rows(0, j), pl.ds(at, step)] = product(
                2 * kw + at, step, low, uq_ref[:, pl.ds(at, step)]
            )
            return carry

        lax.fori_loop(0, qw // step, query_tile, 0)

    def phase(d, carry):
        @pl.when(d > 0)
        def _():
            for c in range(C):
                @pl.when(u + d < H)
                def _():
                    send(u + d, c, 0).wait_recv()

                    @pl.when(u > 0)
                    def _():
                        send(u + d, c, 0).start()

                @pl.when(u - d >= 0)
                def _():
                    send(u - d, c, 1).wait_recv()

                    @pl.when(u < H - 1)
                    def _():
                        send(u - d, c, 1).start()

        def side_step(side, inner):
            j = u + d * (1 - 2 * side)

            @pl.when((j >= 0) & (j < H) & (d + 1 > side))
            def _():
                project(j)

            return inner

        lax.fori_loop(0, jnp.where(d > 0, 2, 1), side_step, 0)
        return carry

    lax.fori_loop(0, H, phase, 0)

    def keys_arrived(j, carry):
        for d in range(1, B):
            @pl.when(b - d >= 0)
            def _():
                kv_copy(j, d).wait_recv()

        return carry

    lax.fori_loop(0, H, keys_arrived, 0)

    groups = kw // HEAD_SIZE
    group = QUERY_HEADS // KEY_VALUE_HEADS
    scale = math.log2(math.e) / math.sqrt(HEAD_SIZE)

    def attend(j):
        at_rows = shard_rows(0, j)
        first = (b * H + j) * rows
        pos = (first + lax.broadcasted_iota(jnp.int32, (rows, 1), 0)).astype(jnp.float32)
        lower = jnp.zeros((rows, 1), jnp.float32)
        for k in range(1, segments):
            lower = jnp.where(pos >= starts[k], starts[k], lower)
        peak[...] = jnp.full_like(peak, MASKED)
        total[...] = jnp.zeros_like(total)
        tiles = (first + rows - 1) // T + 1

        def key_tile(i, inner):
            index = tiles - 1 - i
            at_keys = pl.ds(pl.multiple_of(index * T, T), T)
            key_pos = (index * T + lax.broadcasted_iota(jnp.int32, (rows, T), 1)).astype(
                jnp.float32
            )
            bias = jnp.where((key_pos <= pos) & (key_pos >= lower), 0.0, MASKED)
            bias = jnp.concatenate([bias] * group, axis=0)
            for g in range(groups):
                keys = kv[at_keys, g * HEAD_SIZE : (g + 1) * HEAD_SIZE]
                values = kv[at_keys, (groups + g) * HEAD_SIZE : (groups + g + 1) * HEAD_SIZE]
                values = jnp.concatenate([values, jnp.ones_like(values)], axis=1)
                query = jnp.concatenate(
                    [
                        q_buf[at_rows, h * HEAD_SIZE : (h + 1) * HEAD_SIZE]
                        for h in range(g * group, (g + 1) * group)
                    ],
                    axis=0,
                )
                scores = lax.dot_general(
                    query, keys, (((1,), (1,)), ((), ())), preferred_element_type=jnp.float32
                )
                scores = scores * scale + bias
                before = peak[g]
                fresh = jnp.maximum(before, jnp.max(scores, axis=1, keepdims=True))
                shares = jnp.exp2(scores - fresh[:, :1]).astype(jnp.bfloat16)
                decay = jnp.exp2(before - fresh)
                peak[g] = fresh
                total[g] = total[g] * jnp.concatenate([decay, decay], axis=1) + jnp.dot(
                    shares, values, preferred_element_type=jnp.float32
                )
            return inner

        lax.fori_loop(0, tiles, key_tile, 0)
        for h in range(groups * group):
            g, at = h // group, (h % group) * rows
            left[at_rows, h * HEAD_SIZE : (h + 1) * HEAD_SIZE] = (
                total[g, at : at + rows, :HEAD_SIZE] / total[g, at : at + rows, HEAD_SIZE:]
            ).astype(jnp.bfloat16)
        lows = jnp.dot(
            left[at_rows, :qw], out_down_ref[...], preferred_element_type=jnp.float32
        )
        mask = tenant_mask(starts, adapter_ref, first, rows, HIDDEN)
        lows = jnp.where(mask, adapter_scale * lows, 0.0)
        high = lows.astype(jnp.bfloat16)
        left[at_rows, qw : qw + HIDDEN] = high
        left[at_rows, qw + HIDDEN :] = (lows - high.astype(jnp.float32)).astype(jnp.bfloat16)

    def own_part(j, c):
        columns = pl.ds(pl.multiple_of(c * width, width), width)
        return jnp.dot(
            left[shard_rows(0, j), :], out_weights[:, columns], preferred_element_type=jnp.float32
        )

    def hop(j, c, side):
        return pltpu.make_async_remote_copy(
            src_ref=sent.at[j, c],
            dst_ref=landed.at[side, j, c],
            send_sem=hop_send.at[j, c],
            recv_sem=hop_recv.at[side, j, c],
            device_id=(b, u + 2 * side - 1),
            device_id_type=MESH,
        )

    for copy in output_copies():
        copy.wait()

    def step(p, carry):
        def side_shard(side):
            j = jnp.where(side == 0, p, H - 1 - p)
            return j, jnp.where(side == 0, u - j, j - u) > 0

        def attend_any(side, side_carry):
            j, further = side_shard(side)
            final = p == H - 1

            @pl.when((final & (side == 0)) | ((p < H - 1) & further))
            def _():
                attend(jnp.where(final, u, j))

            return side_carry

        lax.fori_loop(0, 2, attend_any, 0)

        def chunk(c, inner_carry):
            def pass_on(side, side_carry):
                j, further = side_shard(side)
                behind = jnp.where(side == 0, H - 1 - u, u)

                @pl.when(further)
                def _():
                    value = own_part(j, c)

                    @pl.when(behind > 0)
                    def _():
                        hop(j, c, side).wait_recv()
                        sent[j, c] = (value + landed[side, j, c].astype(jnp.float32)).astype(
                            jnp.bfloat16
                        )

                    @pl.when(behind == 0)
                    def _():
                        sent[j, c] = value.astype(jnp.bfloat16)

                    hop(j, c, side).start()

                return side_carry

            lax.fori_loop(0, 2, pass_on, 0)
            return inner_carry

        @pl.when(p < H - 1)
        def _():
            lax.fori_loop(0, D, chunk, 0)

        return carry

    lax.fori_loop(0, H, step, 0)

    def last(c, carry):
        columns = pl.ds(pl.multiple_of(c * width, width), width)
        value = own_part(u, c)

        @pl.when(u > 0)
        def _():
            hop(u, c, 1).wait_recv()

        @pl.when(u < H - 1)
        def _():
            hop(u, c, 0).wait_recv()

        from_left = jnp.where(u > 0, landed[1, u, c].astype(jnp.float32), 0.0)
        from_right = jnp.where(u < H - 1, landed[0, u, c].astype(jnp.float32), 0.0)
        out_ref[:, columns] = (value + from_left + from_right).astype(jnp.bfloat16)
        return carry

    lax.fori_loop(0, D, last, 0)

    def finish(j, carry):
        for c in range(C):
            @pl.when((j >= u) & (u > 0))
            def _():
                send(j, c, 0).wait_send()

            @pl.when((j <= u) & (u < H - 1))
            def _():
                send(j, c, 1).wait_send()

        for d in range(1, B):
            @pl.when(b + d < B)
            def _():
                kv_copy(j, d).wait_send()

        for c in range(D):
            @pl.when(j != u)
            def _():
                hop(j, c, jnp.where(j < u, 0, 1)).wait_send()

        return carry

    lax.fori_loop(0, H, finish, 0)


IN_VMEM = pl.BlockSpec(memory_space=pltpu.VMEM)
IN_SMEM = pl.BlockSpec(memory_space=pltpu.SMEM)
ANYWHERE = pl.BlockSpec(memory_space=pl.ANY)


def shards(
    activations,
    input_norm_gain,
    query_weight,
    key_weight,
    value_weight,
    output_weight,
    adapter_down_maps,
    query_up_maps,
    key_up_maps,
    value_up_maps,
    output_down_maps,
    output_up_maps,
    segment_index,
    segment_adapter,
):
    H = lax.axis_size("uly")
    B = lax.axis_size("blk")
    rows, features = activations.shape
    tokens = segment_index.shape[0]
    segments = segment_adapter.shape[0]
    qw = query_weight.shape[1]
    kw = key_weight.shape[1]
    block_rows = rows * H
    seg = segment_index.reshape(tokens // 128, 128)
    bf16 = jnp.bfloat16
    C, D = 3, 4
    T = math.gcd(tokens, 512)
    group_rows = QUERY_HEADS // KEY_VALUE_HEADS * rows
    groups = kw // HEAD_SIZE
    f32 = jnp.float32
    return pl.pallas_call(
        functools.partial(block_kernel, H, B, C, D, T, segments),
        out_shape=jax.ShapeDtypeStruct((rows, features), bf16),
        in_specs=[IN_VMEM] * 2
        + [ANYWHERE] * 4
        + [IN_VMEM] * 3
        + [ANYWHERE, IN_VMEM, ANYWHERE, IN_VMEM, IN_SMEM],
        out_specs=IN_VMEM,
        scratch_shapes=[
            pltpu.VMEM((H, rows, features), bf16),
            pltpu.VMEM((features, qw + 2 * kw), bf16),
            pltpu.VMEM(adapter_down_maps.shape, bf16),
            pltpu.VMEM((block_rows, qw), bf16),
            pltpu.VMEM((tokens, 2 * kw), bf16),
            pltpu.VMEM((groups, group_rows, HEAD_SIZE), f32),
            pltpu.VMEM((groups, group_rows, 2 * HEAD_SIZE), f32),
            pltpu.VMEM((block_rows, qw + 2 * HIDDEN), bf16),
            pltpu.VMEM((qw + 2 * HIDDEN, features), bf16),
            pltpu.VMEM((H, D, rows, features // D), bf16),
            pltpu.VMEM((2, H, D, rows, features // D), bf16),
            pltpu.SemaphoreType.DMA((4,)),
            pltpu.SemaphoreType.DMA((3,)),
            pltpu.SemaphoreType.DMA((2, H, C)),
            pltpu.SemaphoreType.DMA((H, C)),
            pltpu.SemaphoreType.DMA((B, H)),
            pltpu.SemaphoreType.DMA((B, H)),
            pltpu.SemaphoreType.DMA((H, D)),
            pltpu.SemaphoreType.DMA((2, H, D)),
        ],
        compiler_params=pltpu.CompilerParams(
            collective_id=0, has_side_effects=True, vmem_limit_bytes=VMEM_LIMIT
        ),
        name="attention_block",
    )(
        activations,
        input_norm_gain.reshape(1, features),
        adapter_down_maps,
        query_weight,
        key_weight,
        value_weight,
        query_up_maps,
        key_up_maps,
        value_up_maps,
        output_weight,
        output_down_maps,
        output_up_maps,
        seg,
        segment_adapter,
    )


def solution(mesh):
    return jax.shard_map(
        shards,
        mesh=mesh,
        in_specs=(
            P(("blk", "uly"), None),
            P(),
            P(None, "uly"),
            P(None, "uly"),
            P(None, "uly"),
            P("uly", None),
            P(),
            P(None, "uly"),
            P(None, "uly"),
            P(None, "uly"),
            P("uly", None),
            P(),
            P(),
            P(),
        ),
        out_specs=P(("blk", "uly"), None),
        check_vma=False,
    )
```

```python
import functools
import math

import jax
import jax.numpy as jnp
from jax import lax
from jax.experimental import pallas as pl
from jax.experimental.pallas import tpu as pltpu
from jax.sharding import PartitionSpec as P

QUERY_HEADS = 32
KEY_VALUE_HEADS = 8
HEAD_SIZE = 128
ADAPTER_RANK = 16
ADAPTER_COUNT = 8
HIDDEN = ADAPTER_COUNT * ADAPTER_RANK

eps_norm = 1e-05
adapter_scale = 2.0
MESH = pl.DeviceIdType.MESH
VMEM_LIMIT = 60 * 1024 * 1024
MASKED = -1e30
LAG = 2


def segment_starts(seg_ref, segments):
    seg = seg_ref[...]
    starts = []
    for k in range(segments):
        below = jnp.where(seg < k, 1.0, 0.0)
        starts.append(jnp.sum(jnp.sum(below, axis=1, keepdims=True), axis=0, keepdims=True))
    return starts


def tenant_mask(starts, adapter_ref, first, rows, width):
    pos = (first + lax.broadcasted_iota(jnp.int32, (rows, width), 0)).astype(jnp.float32)
    column = lax.broadcasted_iota(jnp.int32, (rows, width), 1)
    column = (column // ADAPTER_RANK) % ADAPTER_COUNT
    tenant = jnp.zeros((rows, width), jnp.int32) + adapter_ref[0]
    for k in range(1, len(starts)):
        tenant = jnp.where(pos >= starts[k], adapter_ref[k], tenant)
    return column == tenant


def block_kernel(
    H, B, C, D, T, segments,
    x_ref, gain_ref, down_ref, wq_ref, wk_ref, wv_ref, uq_ref, uk_ref, uv_ref,
    wo_ref, out_down_ref, out_up_ref, seg_ref, adapter_ref,
    out_ref,
    rows_buf, weights, down, q_buf, kv, peak, total, left, out_weights, sent, landed,
    w_sem, o_sem, send_sem, recv_sem, kv_send, kv_recv, hop_send, hop_recv,
):
    u = lax.axis_index("uly")
    b = lax.axis_index("blk")
    rows, features = x_ref.shape
    part = rows // C
    kw = wk_ref.shape[1]
    qw = wq_ref.shape[1]
    width = features // D

    def weight_copies():
        return [
            pltpu.make_async_copy(down_ref, down, w_sem.at[0]),
            pltpu.make_async_copy(wk_ref, weights.at[:, pl.ds(0, kw)], w_sem.at[1]),
            pltpu.make_async_copy(wv_ref, weights.at[:, pl.ds(kw, kw)], w_sem.at[2]),
            pltpu.make_async_copy(wq_ref, weights.at[:, pl.ds(2 * kw, qw)], w_sem.at[3]),
        ]

    def output_copies():
        return [
            pltpu.make_async_copy(wo_ref, out_weights.at[pl.ds(0, qw), :], o_sem.at[0]),
            pltpu.make_async_copy(
                out_up_ref, out_weights.at[pl.ds(qw, HIDDEN), :], o_sem.at[1]
            ),
            pltpu.make_async_copy(
                out_up_ref, out_weights.at[pl.ds(qw + HIDDEN, HIDDEN), :], o_sem.at[2]
            ),
        ]

    for copy in weight_copies():
        copy.start()
    kv[...] = jnp.zeros_like(kv)

    barrier = pltpu.get_barrier_semaphore()

    @pl.when(u > 0)
    def _():
        pl.semaphore_signal(barrier, inc=1, device_id=(b, u - 1), device_id_type=MESH)

    @pl.when(u < H - 1)
    def _():
        pl.semaphore_signal(barrier, inc=1, device_id=(b, u + 1), device_id_type=MESH)

    for d in range(1, B):
        pl.semaphore_signal(
            barrier, inc=1, device_id=(lax.rem(b + d, B), u), device_id_type=MESH
        )

    def send(j, c, side):
        where = rows_buf.at[j, pl.ds(c * part, part), :]
        return pltpu.make_async_remote_copy(
            src_ref=where,
            dst_ref=where,
            send_sem=send_sem.at[side, j, c],
            recv_sem=recv_sem.at[j, c],
            device_id=(b, u - 1 if side == 0 else u + 1),
            device_id_type=MESH,
        )

    def send_if(j, c):
        @pl.when((j >= u) & (u > 0))
        def _():
            send(j, c, 0).start()

        @pl.when((j <= u) & (u < H - 1))
        def _():
            send(j, c, 1).start()

    def normalize(c):
        values = x_ref[pl.ds(c * part, part), :].astype(jnp.float32)
        power = jnp.mean(values * values, axis=1, keepdims=True)
        normed = values * lax.rsqrt(power + eps_norm) * gain_ref[...]
        rows_buf[u, pl.ds(c * part, part), :] = normed.astype(jnp.bfloat16)

    normalize(0)

    @pl.when((u > 0) & (u < H - 1))
    def _():
        pl.semaphore_wait(barrier, B + 1)

    @pl.when((u == 0) | (u == H - 1))
    def _():
        pl.semaphore_wait(barrier, B)

    send_if(u, 0)
    for c in range(1, C):
        normalize(c)
        send_if(u, c)

    starts = segment_starts(seg_ref, segments)
    for copy in weight_copies():
        copy.wait()
    for copy in output_copies():
        copy.start()

    def shard_rows(block, j):
        return pl.ds(pl.multiple_of((block * H + j) * rows, rows), rows)

    def kv_copy(j, d):
        where = kv.at[shard_rows(b, j), :]
        return pltpu.make_async_remote_copy(
            src_ref=where,
            dst_ref=where,
            send_sem=kv_send.at[d, j],
            recv_sem=kv_recv.at[d, j],
            device_id=(b + d, u),
            device_id_type=MESH,
        )

    def project(j):
        shard = rows_buf[j]
        mask = tenant_mask(starts, adapter_ref, (b * H + j) * rows, rows, HIDDEN)

        def lowered(which):
            raw = jnp.dot(
                shard,
                down[:, which * HIDDEN : (which + 1) * HIDDEN],
                preferred_element_type=jnp.float32,
            )
            return jnp.where(mask, raw, 0.0).astype(jnp.bfloat16)

        def product(column, width, low, up):
            return (
                jnp.dot(
                    shard, weights[:, pl.ds(column, width)], preferred_element_type=jnp.float32
                )
                + adapter_scale * jnp.dot(low, up, preferred_element_type=jnp.float32)
            ).astype(jnp.bfloat16)

        kv[shard_rows(b, j), :kw] = product(0, kw, lowered(1), uk_ref[...])
        kv[shard_rows(b, j), kw:] = product(kw, kw, lowered(2), uv_ref[...])
        for d in range(1, B):
            @pl.when(b + d < B)
            def _():
                kv_copy(j, d).start()

        low = lowered(0)
        step = 256

        def query_tile(n, carry):
            at = pl.multiple_of(n * step, step)
            q_buf[shard_rows(0, j), pl.ds(at, step)] = product(
                2 * kw + at, step, low, uq_ref[:, pl.ds(at, step)]
            )
            return carry

        lax.fori_loop(0, qw // step, query_tile, 0)

    def phase(d, carry):
        @pl.when(d > 0)
        def _():
            for c in range(C):
                @pl.when(u + d < H)
                def _():
                    send(u + d, c, 0).wait_recv()

                    @pl.when(u > 0)
                    def _():
                        send(u + d, c, 0).start()

                @pl.when(u - d >= 0)
                def _():
                    send(u - d, c, 1).wait_recv()

                    @pl.when(u < H - 1)
                    def _():
                        send(u - d, c, 1).start()

        def side_step(side, inner):
            j = u + d * (1 - 2 * side)

            @pl.when((j >= 0) & (j < H) & (d + 1 > side))
            def _():
                project(j)

            return inner

        lax.fori_loop(0, jnp.where(d > 0, 2, 1), side_step, 0)
        return carry

    lax.fori_loop(0, H, phase, 0)

    def keys_arrived(j, carry):
        for d in range(1, B):
            @pl.when(b - d >= 0)
            def _():
                kv_copy(j, d).wait_recv()

        return carry

    lax.fori_loop(0, H, keys_arrived, 0)

    groups = kw // HEAD_SIZE
    group = QUERY_HEADS // KEY_VALUE_HEADS
    scale = math.log2(math.e) / math.sqrt(HEAD_SIZE)

    def attend(j):
        at_rows = shard_rows(0, j)
        first = (b * H + j) * rows
        pos = (first + lax.broadcasted_iota(jnp.int32, (rows, 1), 0)).astype(jnp.float32)
        lower = jnp.zeros((rows, 1), jnp.float32)
        for k in range(1, segments):
            lower = jnp.where(pos >= starts[k], starts[k], lower)
        peak[...] = jnp.full_like(peak, MASKED)
        total[...] = jnp.zeros_like(total)
        tiles = (first + rows - 1) // T + 1

        def key_tile(i, inner):
            index = tiles - 1 - i
            at_keys = pl.ds(pl.multiple_of(index * T, T), T)
            key_pos = (index * T + lax.broadcasted_iota(jnp.int32, (rows, T), 1)).astype(
                jnp.float32
            )
            bias = jnp.where((key_pos <= pos) & (key_pos >= lower), 0.0, MASKED)
            for g in range(groups):
                keys = kv[at_keys, g * HEAD_SIZE : (g + 1) * HEAD_SIZE]
                values = kv[at_keys, (groups + g) * HEAD_SIZE : (groups + g + 1) * HEAD_SIZE]
                values = jnp.concatenate([values, jnp.ones_like(values)], axis=1)
                query = jnp.concatenate(
                    [
                        q_buf[at_rows, h * HEAD_SIZE : (h + 1) * HEAD_SIZE]
                        for h in range(g * group, (g + 1) * group)
                    ],
                    axis=0,
                )
                scores = lax.dot_general(
                    query, keys, (((1,), (1,)), ((), ())), preferred_element_type=jnp.float32
                )
                scores = scores.reshape(group, rows, T) * scale + bias[None]
                scores = scores.reshape(group * rows, T)
                before = peak[g]
                fresh = jnp.maximum(before, jnp.max(scores, axis=1, keepdims=True))
                shares = jnp.exp2(scores - fresh[:, :1]).astype(jnp.bfloat16)
                decay = jnp.exp2(before - fresh)
                peak[g] = fresh
                total[g] = total[g] * jnp.concatenate([decay, decay], axis=1) + jnp.dot(
                    shares, values, preferred_element_type=jnp.float32
                )
            return inner

        lax.fori_loop(0, tiles, key_tile, 0)
        for h in range(groups * group):
            g, at = h // group, (h % group) * rows
            left[at_rows, h * HEAD_SIZE : (h + 1) * HEAD_SIZE] = (
                total[g, at : at + rows, :HEAD_SIZE] / total[g, at : at + rows, HEAD_SIZE:]
            ).astype(jnp.bfloat16)
        lows = jnp.dot(
            left[at_rows, :qw], out_down_ref[...], preferred_element_type=jnp.float32
        )
        mask = tenant_mask(starts, adapter_ref, first, rows, HIDDEN)
        lows = jnp.where(mask, adapter_scale * lows, 0.0)
        high = lows.astype(jnp.bfloat16)
        left[at_rows, qw : qw + HIDDEN] = high
        left[at_rows, qw + HIDDEN :] = (lows - high.astype(jnp.float32)).astype(jnp.bfloat16)

    def own_part(j, c):
        columns = pl.ds(pl.multiple_of(c * width, width), width)
        return jnp.dot(
            left[shard_rows(0, j), :], out_weights[:, columns], preferred_element_type=jnp.float32
        )

    def hop(j, c, side):
        return pltpu.make_async_remote_copy(
            src_ref=sent.at[j, c],
            dst_ref=landed.at[side, j, c],
            send_sem=hop_send.at[j, c],
            recv_sem=hop_recv.at[side, j, c],
            device_id=(b, u + 2 * side - 1),
            device_id_type=MESH,
        )

    for copy in output_copies():
        copy.wait()

    hops = (H - 1) * D
    final = 1 + hops + LAG * (H - 2)

    def place(n, side):
        p = n // D
        j = jnp.where(side == 0, p, H - 1 - p)
        sends = jnp.where(side == 0, u - j, j - u) > 0
        return j, n % D, sends

    def step(t, carry):
        def position(side):
            behind = jnp.where(side == 0, H - 1 - u, u)
            n = t - 1 - LAG * jnp.maximum(behind - 1, 0)
            return jnp.clip(n, 0, hops - 1), (n >= 0) & (n < hops), behind

        def attend_side(side, side_carry):
            n, inside, _ = position(side)
            j, c, sends = place(jnp.where(t == 0, 0, n), side)
            due = (t == 0) | (inside & (c == 0) & (n > 0))

            @pl.when(((t < final) & sends & due) | ((t == final) & (side == 0)))
            def _():
                attend(jnp.where(t == final, u, j))

            return side_carry

        lax.fori_loop(0, 2, attend_side, 0)

        def pass_on(side, side_carry):
            n, inside, behind = position(side)
            j, c, sends = place(n, side)

            @pl.when(inside & sends)
            def _():
                value = own_part(j, c)

                @pl.when(behind > 0)
                def _():
                    hop(j, c, side).wait_recv()
                    sent[j, c] = (value + landed[side, j, c].astype(jnp.float32)).astype(
                        jnp.bfloat16
                    )

                @pl.when(behind == 0)
                def _():
                    sent[j, c] = value.astype(jnp.bfloat16)

                hop(j, c, side).start()

            return side_carry

        lax.fori_loop(0, 2, pass_on, 0)
        return carry

    lax.fori_loop(0, final + 1, step, 0)

    def last(c, carry):
        columns = pl.ds(pl.multiple_of(c * width, width), width)
        value = own_part(u, c)

        @pl.when(u > 0)
        def _():
            hop(u, c, 1).wait_recv()

        @pl.when(u < H - 1)
        def _():
            hop(u, c, 0).wait_recv()

        from_left = jnp.where(u > 0, landed[1, u, c].astype(jnp.float32), 0.0)
        from_right = jnp.where(u < H - 1, landed[0, u, c].astype(jnp.float32), 0.0)
        out_ref[:, columns] = (value + from_left + from_right).astype(jnp.bfloat16)
        return carry

    lax.fori_loop(0, D, last, 0)

    def finish(j, carry):
        for c in range(C):
            @pl.when((j >= u) & (u > 0))
            def _():
                send(j, c, 0).wait_send()

            @pl.when((j <= u) & (u < H - 1))
            def _():
                send(j, c, 1).wait_send()

        for d in range(1, B):
            @pl.when(b + d < B)
            def _():
                kv_copy(j, d).wait_send()

        for c in range(D):
            @pl.when(j != u)
            def _():
                hop(j, c, jnp.where(j < u, 0, 1)).wait_send()

        return carry

    lax.fori_loop(0, H, finish, 0)


IN_VMEM = pl.BlockSpec(memory_space=pltpu.VMEM)
IN_SMEM = pl.BlockSpec(memory_space=pltpu.SMEM)
ANYWHERE = pl.BlockSpec(memory_space=pl.ANY)


def shards(
    activations,
    input_norm_gain,
    query_weight,
    key_weight,
    value_weight,
    output_weight,
    adapter_down_maps,
    query_up_maps,
    key_up_maps,
    value_up_maps,
    output_down_maps,
    output_up_maps,
    segment_index,
    segment_adapter,
):
    H = lax.axis_size("uly")
    B = lax.axis_size("blk")
    rows, features = activations.shape
    tokens = segment_index.shape[0]
    segments = segment_adapter.shape[0]
    qw = query_weight.shape[1]
    kw = key_weight.shape[1]
    block_rows = rows * H
    seg = segment_index.reshape(tokens // 128, 128)
    bf16 = jnp.bfloat16
    C, D = 3, 4
    T = math.gcd(tokens, 1024)
    group_rows = QUERY_HEADS // KEY_VALUE_HEADS * rows
    groups = kw // HEAD_SIZE
    f32 = jnp.float32
    return pl.pallas_call(
        functools.partial(block_kernel, H, B, C, D, T, segments),
        out_shape=jax.ShapeDtypeStruct((rows, features), bf16),
        in_specs=[IN_VMEM] * 2
        + [ANYWHERE] * 4
        + [IN_VMEM] * 3
        + [ANYWHERE, IN_VMEM, ANYWHERE, IN_VMEM, IN_SMEM],
        out_specs=IN_VMEM,
        scratch_shapes=[
            pltpu.VMEM((H, rows, features), bf16),
            pltpu.VMEM((features, qw + 2 * kw), bf16),
            pltpu.VMEM(adapter_down_maps.shape, bf16),
            pltpu.VMEM((block_rows, qw), bf16),
            pltpu.VMEM((tokens, 2 * kw), bf16),
            pltpu.VMEM((groups, group_rows, HEAD_SIZE), f32),
            pltpu.VMEM((groups, group_rows, 2 * HEAD_SIZE), f32),
            pltpu.VMEM((block_rows, qw + 2 * HIDDEN), bf16),
            pltpu.VMEM((qw + 2 * HIDDEN, features), bf16),
            pltpu.VMEM((H, D, rows, features // D), bf16),
            pltpu.VMEM((2, H, D, rows, features // D), bf16),
            pltpu.SemaphoreType.DMA((4,)),
            pltpu.SemaphoreType.DMA((3,)),
            pltpu.SemaphoreType.DMA((2, H, C)),
            pltpu.SemaphoreType.DMA((H, C)),
            pltpu.SemaphoreType.DMA((B, H)),
            pltpu.SemaphoreType.DMA((B, H)),
            pltpu.SemaphoreType.DMA((H, D)),
            pltpu.SemaphoreType.DMA((2, H, D)),
        ],
        compiler_params=pltpu.CompilerParams(
            collective_id=0, has_side_effects=True, vmem_limit_bytes=VMEM_LIMIT
        ),
        name="attention_block",
    )(
        activations,
        input_norm_gain.reshape(1, features),
        adapter_down_maps,
        query_weight,
        key_weight,
        value_weight,
        query_up_maps,
        key_up_maps,
        value_up_maps,
        output_weight,
        output_down_maps,
        output_up_maps,
        seg,
        segment_adapter,
    )


def solution(mesh):
    return jax.shard_map(
        shards,
        mesh=mesh,
        in_specs=(
            P(("blk", "uly"), None),
            P(),
            P(None, "uly"),
            P(None, "uly"),
            P(None, "uly"),
            P("uly", None),
            P(),
            P(None, "uly"),
            P(None, "uly"),
            P(None, "uly"),
            P("uly", None),
            P(),
            P(),
            P(),
        ),
        out_specs=P(("blk", "uly"), None),
        check_vma=False,
    )
```

```python
import functools
import math

import jax
import jax.numpy as jnp
import numpy as np
from jax import lax
from jax.experimental import pallas as pl
from jax.experimental.pallas import tpu as pltpu
from jax.sharding import PartitionSpec as P

QUERY_HEADS = 32
KEY_VALUE_HEADS = 8
HEAD_SIZE = 128
ADAPTER_RANK = 16
ADAPTER_COUNT = 8
HIDDEN = ADAPTER_COUNT * ADAPTER_RANK

eps_norm = 1e-05
adapter_scale = 2.0
MESH = pl.DeviceIdType.MESH
VMEM_LIMIT = 60 * 1024 * 1024
MASKED = -1e30
LAG = 2


def segment_starts(seg_ref, segments):
    seg = seg_ref[...]
    starts = []
    for k in range(segments):
        below = jnp.where(seg < k, 1.0, 0.0)
        starts.append(jnp.sum(jnp.sum(below, axis=1, keepdims=True), axis=0, keepdims=True))
    return starts


def tenant_mask(starts, adapter_ref, first, rows, width):
    pos = (first + lax.broadcasted_iota(jnp.int32, (rows, width), 0)).astype(jnp.float32)
    column = lax.broadcasted_iota(jnp.int32, (rows, width), 1)
    column = (column // ADAPTER_RANK) % ADAPTER_COUNT
    tenant = jnp.zeros((rows, width), jnp.int32) + adapter_ref[0]
    for k in range(1, len(starts)):
        tenant = jnp.where(pos >= starts[k], adapter_ref[k], tenant)
    return column == tenant


def block_kernel(
    H, B, C, D, segments,
    x_ref, gain_ref, down_ref, wq_ref, wk_ref, wv_ref, uq_ref, uk_ref, uv_ref,
    wo_ref, out_down_ref, out_up_ref, seg_ref, key_pos_ref, adapter_ref,
    out_ref,
    rows_buf, weights, down, q_buf, kv, peak, total, left, out_weights, sent, landed,
    w_sem, o_sem, send_sem, recv_sem, kv_send, kv_recv, hop_send, hop_recv,
):
    u = lax.axis_index("uly")
    b = lax.axis_index("blk")
    rows, features = x_ref.shape
    part = rows // C
    kw = wk_ref.shape[1]
    qw = wq_ref.shape[1]
    width = features // D

    def weight_copies():
        return [
            pltpu.make_async_copy(down_ref, down, w_sem.at[0]),
            pltpu.make_async_copy(wk_ref, weights.at[:, pl.ds(0, kw)], w_sem.at[1]),
            pltpu.make_async_copy(wv_ref, weights.at[:, pl.ds(kw, kw)], w_sem.at[2]),
            pltpu.make_async_copy(wq_ref, weights.at[:, pl.ds(2 * kw, qw)], w_sem.at[3]),
        ]

    def output_copies():
        return [
            pltpu.make_async_copy(wo_ref, out_weights.at[pl.ds(0, qw), :], o_sem.at[0]),
            pltpu.make_async_copy(
                out_up_ref, out_weights.at[pl.ds(qw, HIDDEN), :], o_sem.at[1]
            ),
            pltpu.make_async_copy(
                out_up_ref, out_weights.at[pl.ds(qw + HIDDEN, HIDDEN), :], o_sem.at[2]
            ),
        ]

    for copy in weight_copies():
        copy.start()
    kv[...] = jnp.zeros_like(kv)

    barrier = pltpu.get_barrier_semaphore()

    @pl.when(u > 0)
    def _():
        pl.semaphore_signal(barrier, inc=1, device_id=(b, u - 1), device_id_type=MESH)

    @pl.when(u < H - 1)
    def _():
        pl.semaphore_signal(barrier, inc=1, device_id=(b, u + 1), device_id_type=MESH)

    for d in range(1, B):
        pl.semaphore_signal(
            barrier, inc=1, device_id=(lax.rem(b + d, B), u), device_id_type=MESH
        )

    def send(j, c, side):
        where = rows_buf.at[j, pl.ds(c * part, part), :]
        return pltpu.make_async_remote_copy(
            src_ref=where,
            dst_ref=where,
            send_sem=send_sem.at[side, j, c],
            recv_sem=recv_sem.at[j, c],
            device_id=(b, u - 1 if side == 0 else u + 1),
            device_id_type=MESH,
        )

    def send_if(j, c):
        @pl.when((j >= u) & (u > 0))
        def _():
            send(j, c, 0).start()

        @pl.when((j <= u) & (u < H - 1))
        def _():
            send(j, c, 1).start()

    def normalize(c):
        values = x_ref[pl.ds(c * part, part), :].astype(jnp.float32)
        power = jnp.mean(values * values, axis=1, keepdims=True)
        normed = values * lax.rsqrt(power + eps_norm) * gain_ref[...]
        rows_buf[u, pl.ds(c * part, part), :] = normed.astype(jnp.bfloat16)

    normalize(0)

    @pl.when((u > 0) & (u < H - 1))
    def _():
        pl.semaphore_wait(barrier, B + 1)

    @pl.when((u == 0) | (u == H - 1))
    def _():
        pl.semaphore_wait(barrier, B)

    send_if(u, 0)
    for c in range(1, C):
        normalize(c)
        send_if(u, c)

    starts = segment_starts(seg_ref, segments)
    for copy in weight_copies():
        copy.wait()
    for copy in output_copies():
        copy.start()

    def shard_rows(j):
        return pl.ds(pl.multiple_of(j * rows, rows), rows)

    def key_rows(block, j):
        return pl.ds(pl.multiple_of((j * B + block) * rows, rows), rows)

    def kv_copy(j, d):
        where = kv.at[key_rows(b, j), :]
        return pltpu.make_async_remote_copy(
            src_ref=where,
            dst_ref=where,
            send_sem=kv_send.at[d, j],
            recv_sem=kv_recv.at[d, j],
            device_id=(b + d, u),
            device_id_type=MESH,
        )

    def project(j):
        shard = rows_buf[j]
        mask = tenant_mask(starts, adapter_ref, (b * H + j) * rows, rows, HIDDEN)

        def lowered(which):
            raw = jnp.dot(
                shard,
                down[:, which * HIDDEN : (which + 1) * HIDDEN],
                preferred_element_type=jnp.float32,
            )
            return jnp.where(mask, raw, 0.0).astype(jnp.bfloat16)

        def product(column, width, low, up):
            return (
                jnp.dot(
                    shard, weights[:, pl.ds(column, width)], preferred_element_type=jnp.float32
                )
                + adapter_scale * jnp.dot(low, up, preferred_element_type=jnp.float32)
            ).astype(jnp.bfloat16)

        kv[key_rows(b, j), :kw] = product(0, kw, lowered(1), uk_ref[...])
        kv[key_rows(b, j), kw:] = product(kw, kw, lowered(2), uv_ref[...])
        for d in range(1, B):
            @pl.when(b + d < B)
            def _():
                kv_copy(j, d).start()

        low = lowered(0)
        step = 256

        def query_tile(n, carry):
            at = pl.multiple_of(n * step, step)
            q_buf[shard_rows(j), pl.ds(at, step)] = product(
                2 * kw + at, step, low, uq_ref[:, pl.ds(at, step)]
            )
            return carry

        lax.fori_loop(0, qw // step, query_tile, 0)

    at_end = (u == 0) | (u == H - 1)

    def await_keys(known):
        def keys_arrived(j, carry):
            early = at_end & (j != H - 1 - u)
            for d in range(1, B):
                @pl.when((b - d >= 0) & (early if known else jnp.logical_not(early)))
                def _():
                    kv_copy(j, d).wait_recv()

            return carry

        lax.fori_loop(0, H, keys_arrived, 0)

    groups = kw // HEAD_SIZE
    group = QUERY_HEADS // KEY_VALUE_HEADS
    scale = math.log2(math.e) / math.sqrt(HEAD_SIZE)

    T = B * rows
    first_left = jnp.where(u > 1, 1, 0)
    first_right = jnp.where(u < H - 2, H - 2, H - 1)

    def clear():
        peak[...] = jnp.full_like(peak, MASKED)
        total[...] = jnp.zeros_like(total)

    def visit(j, needed):
        at_rows = shard_rows(j)
        first = (b * H + j) * rows
        pos = (first + lax.broadcasted_iota(jnp.int32, (rows, 1), 0)).astype(jnp.float32)
        lower = jnp.zeros((rows, 1), jnp.float32)
        for k in range(1, segments):
            lower = jnp.where(pos >= starts[k], starts[k], lower)

        def key_tile(index):
            at_keys = pl.ds(pl.multiple_of(index * T, T), T)
            key_pos = key_pos_ref[...] + (index * rows).astype(jnp.float32)
            bias = jnp.where((key_pos <= pos) & (key_pos >= lower), 0.0, MASKED)
            for g in range(groups):
                keys = kv[at_keys, g * HEAD_SIZE : (g + 1) * HEAD_SIZE]
                values = kv[at_keys, (groups + g) * HEAD_SIZE : (groups + g + 1) * HEAD_SIZE]
                values = jnp.concatenate([values, jnp.ones_like(values)], axis=1)
                query = jnp.concatenate(
                    [
                        q_buf[at_rows, h * HEAD_SIZE : (h + 1) * HEAD_SIZE]
                        for h in range(g * group, (g + 1) * group)
                    ],
                    axis=0,
                )
                scores = lax.dot_general(
                    query, keys, (((1,), (1,)), ((), ())), preferred_element_type=jnp.float32
                )
                scores = scores.reshape(group, rows, T) * scale + bias[None]
                scores = scores.reshape(group * rows, T)
                before = peak[g]
                fresh = jnp.maximum(before, jnp.max(scores, axis=1, keepdims=True))
                shares = jnp.exp2(scores - fresh[:, :1]).astype(jnp.bfloat16)
                decay = jnp.exp2(before - fresh)
                peak[g] = fresh
                total[g] = total[g] * jnp.concatenate([decay, decay], axis=1) + jnp.dot(
                    shares, values, preferred_element_type=jnp.float32
                )

        def maybe(index, inner):
            @pl.when(needed(index))
            def _():
                key_tile(index)

            return inner

        lax.fori_loop(0, H, maybe, 0)

    def conclude(j):
        at_rows = shard_rows(j)
        first = (b * H + j) * rows
        for h in range(groups * group):
            g, at = h // group, (h % group) * rows
            left[at_rows, h * HEAD_SIZE : (h + 1) * HEAD_SIZE] = (
                total[g, at : at + rows, :HEAD_SIZE] / total[g, at : at + rows, HEAD_SIZE:]
            ).astype(jnp.bfloat16)
        lows = jnp.dot(
            left[at_rows, :qw], out_down_ref[...], preferred_element_type=jnp.float32
        )
        mask = tenant_mask(starts, adapter_ref, first, rows, HIDDEN)
        lows = jnp.where(mask, adapter_scale * lows, 0.0)
        high = lows.astype(jnp.bfloat16)
        left[at_rows, qw : qw + HIDDEN] = high
        left[at_rows, qw + HIDDEN :] = (lows - high.astype(jnp.float32)).astype(jnp.bfloat16)

    def phase(d, carry):
        @pl.when((d == H - 1) & at_end)
        def _():
            await_keys(True)
            clear()
            visit(jnp.where(u == 0, first_right, first_left), lambda s: s != H - 1 - u)

        @pl.when(d > 0)
        def _():
            for c in range(C):
                @pl.when(u + d < H)
                def _():
                    send(u + d, c, 0).wait_recv()

                    @pl.when(u > 0)
                    def _():
                        send(u + d, c, 0).start()

                @pl.when(u - d >= 0)
                def _():
                    send(u - d, c, 1).wait_recv()

                    @pl.when(u < H - 1)
                    def _():
                        send(u - d, c, 1).start()

        def side_step(side, inner):
            j = u + d * (1 - 2 * side)

            @pl.when((j >= 0) & (j < H) & (d + 1 > side))
            def _():
                project(j)

            return inner

        lax.fori_loop(0, jnp.where(d > 0, 2, 1), side_step, 0)
        return carry

    lax.fori_loop(0, H, phase, 0)

    await_keys(False)

    def own_part(j, c):
        columns = pl.ds(pl.multiple_of(c * width, width), width)
        return jnp.dot(
            left[shard_rows(j), :], out_weights[:, columns], preferred_element_type=jnp.float32
        )

    def hop(j, c, side):
        return pltpu.make_async_remote_copy(
            src_ref=sent.at[j, c],
            dst_ref=landed.at[side, j, c],
            send_sem=hop_send.at[j, c],
            recv_sem=hop_recv.at[side, j, c],
            device_id=(b, u + 2 * side - 1),
            device_id_type=MESH,
        )

    for copy in output_copies():
        copy.wait()

    hops = (H - 1) * D
    final = 1 + hops + LAG * (H - 2)

    def place(n, side):
        p = n // D
        p = jnp.where(p < 2, 1 - p, p)
        j = jnp.where(side == 0, p, H - 1 - p)
        sends = jnp.where(side == 0, u - j, j - u) > 0
        return j, n % D, sends

    def step(t, carry):
        def position(side):
            behind = jnp.where(side == 0, H - 1 - u, u)
            n = t - 1 - LAG * jnp.maximum(behind - 1, 0)
            return jnp.clip(n, 0, hops - 1), (n >= 0) & (n < hops), behind

        def attend_side(side, side_carry):
            n, inside, _ = position(side)
            j, c, sends = place(n, side)
            started = jnp.where(side == 0, first_left, first_right)
            opens = jnp.where(side == 0, u, H - 1 - u) > 0
            due = inside & (c == 0) & sends & (j != started)

            @pl.when(((t == 0) & opens) | ((t < final) & due) | ((t == final) & (side == 0)))
            def _():
                shard = jnp.where(t == 0, started, jnp.where(t == final, u, j))
                resumed = (t == 0) & at_end

                @pl.when(jnp.logical_not(resumed))
                def _():
                    clear()

                visit(shard, lambda s: (s == H - 1 - u) | jnp.logical_not(resumed))
                conclude(shard)

            return side_carry

        lax.fori_loop(0, 2, attend_side, 0)

        def pass_on(side, side_carry):
            n, inside, behind = position(side)
            j, c, sends = place(n, side)

            @pl.when(inside & sends)
            def _():
                value = own_part(j, c)

                @pl.when(behind > 0)
                def _():
                    hop(j, c, side).wait_recv()
                    sent[j, c] = (value + landed[side, j, c].astype(jnp.float32)).astype(
                        jnp.bfloat16
                    )

                @pl.when(behind == 0)
                def _():
                    sent[j, c] = value.astype(jnp.bfloat16)

                hop(j, c, side).start()

            return side_carry

        lax.fori_loop(0, 2, pass_on, 0)
        return carry

    lax.fori_loop(0, final + 1, step, 0)

    def last(c, carry):
        columns = pl.ds(pl.multiple_of(c * width, width), width)
        value = own_part(u, c)

        @pl.when(u > 0)
        def _():
            hop(u, c, 1).wait_recv()

        @pl.when(u < H - 1)
        def _():
            hop(u, c, 0).wait_recv()

        from_left = jnp.where(u > 0, landed[1, u, c].astype(jnp.float32), 0.0)
        from_right = jnp.where(u < H - 1, landed[0, u, c].astype(jnp.float32), 0.0)
        out_ref[:, columns] = (value + from_left + from_right).astype(jnp.bfloat16)
        return carry

    lax.fori_loop(0, D, last, 0)

    def finish(j, carry):
        for c in range(C):
            @pl.when((j >= u) & (u > 0))
            def _():
                send(j, c, 0).wait_send()

            @pl.when((j <= u) & (u < H - 1))
            def _():
                send(j, c, 1).wait_send()

        for d in range(1, B):
            @pl.when(b + d < B)
            def _():
                kv_copy(j, d).wait_send()

        for c in range(D):
            @pl.when(j != u)
            def _():
                hop(j, c, jnp.where(j < u, 0, 1)).wait_send()

        return carry

    lax.fori_loop(0, H, finish, 0)


IN_VMEM = pl.BlockSpec(memory_space=pltpu.VMEM)
IN_SMEM = pl.BlockSpec(memory_space=pltpu.SMEM)
ANYWHERE = pl.BlockSpec(memory_space=pl.ANY)


def shards(
    activations,
    input_norm_gain,
    query_weight,
    key_weight,
    value_weight,
    output_weight,
    adapter_down_maps,
    query_up_maps,
    key_up_maps,
    value_up_maps,
    output_down_maps,
    output_up_maps,
    segment_index,
    segment_adapter,
):
    H = lax.axis_size("uly")
    B = lax.axis_size("blk")
    rows, features = activations.shape
    tokens = segment_index.shape[0]
    segments = segment_adapter.shape[0]
    qw = query_weight.shape[1]
    kw = key_weight.shape[1]
    block_rows = rows * H
    seg = segment_index.reshape(tokens // 128, 128)
    bf16 = jnp.bfloat16
    C, D = 3, 4
    key_pos = np.arange(B)[:, None] * block_rows + np.arange(rows)[None, :]
    key_pos = jnp.asarray(key_pos.reshape(1, B * rows), jnp.float32)
    group_rows = QUERY_HEADS // KEY_VALUE_HEADS * rows
    groups = kw // HEAD_SIZE
    f32 = jnp.float32
    return pl.pallas_call(
        functools.partial(block_kernel, H, B, C, D, segments),
        out_shape=jax.ShapeDtypeStruct((rows, features), bf16),
        in_specs=[IN_VMEM] * 2
        + [ANYWHERE] * 4
        + [IN_VMEM] * 3
        + [ANYWHERE, IN_VMEM, ANYWHERE, IN_VMEM, IN_VMEM, IN_SMEM],
        out_specs=IN_VMEM,
        scratch_shapes=[
            pltpu.VMEM((H, rows, features), bf16),
            pltpu.VMEM((features, qw + 2 * kw), bf16),
            pltpu.VMEM(adapter_down_maps.shape, bf16),
            pltpu.VMEM((block_rows, qw), bf16),
            pltpu.VMEM((tokens, 2 * kw), bf16),
            pltpu.VMEM((groups, group_rows, HEAD_SIZE), f32),
            pltpu.VMEM((groups, group_rows, 2 * HEAD_SIZE), f32),
            pltpu.VMEM((block_rows, qw + 2 * HIDDEN), bf16),
            pltpu.VMEM((qw + 2 * HIDDEN, features), bf16),
            pltpu.VMEM((H, D, rows, features // D), bf16),
            pltpu.VMEM((2, H, D, rows, features // D), bf16),
            pltpu.SemaphoreType.DMA((4,)),
            pltpu.SemaphoreType.DMA((3,)),
            pltpu.SemaphoreType.DMA((2, H, C)),
            pltpu.SemaphoreType.DMA((H, C)),
            pltpu.SemaphoreType.DMA((B, H)),
            pltpu.SemaphoreType.DMA((B, H)),
            pltpu.SemaphoreType.DMA((H, D)),
            pltpu.SemaphoreType.DMA((2, H, D)),
        ],
        compiler_params=pltpu.CompilerParams(
            collective_id=0, has_side_effects=True, vmem_limit_bytes=VMEM_LIMIT
        ),
        name="attention_block",
    )(
        activations,
        input_norm_gain.reshape(1, features),
        adapter_down_maps,
        query_weight,
        key_weight,
        value_weight,
        query_up_maps,
        key_up_maps,
        value_up_maps,
        output_weight,
        output_down_maps,
        output_up_maps,
        seg,
        key_pos,
        segment_adapter,
    )


def solution(mesh):
    return jax.shard_map(
        shards,
        mesh=mesh,
        in_specs=(
            P(("blk", "uly"), None),
            P(),
            P(None, "uly"),
            P(None, "uly"),
            P(None, "uly"),
            P("uly", None),
            P(),
            P(None, "uly"),
            P(None, "uly"),
            P(None, "uly"),
            P("uly", None),
            P(),
            P(),
            P(),
        ),
        out_specs=P(("blk", "uly"), None),
        check_vma=False,
    )
```

```python
import functools
import math

import jax
import jax.numpy as jnp
import numpy as np
from jax import lax
from jax.experimental import pallas as pl
from jax.experimental.pallas import tpu as pltpu
from jax.sharding import PartitionSpec as P

QUERY_HEADS = 32
KEY_VALUE_HEADS = 8
HEAD_SIZE = 128
ADAPTER_RANK = 16
ADAPTER_COUNT = 8
HIDDEN = ADAPTER_COUNT * ADAPTER_RANK

eps_norm = 1e-05
adapter_scale = 2.0
MESH = pl.DeviceIdType.MESH
VMEM_LIMIT = 60 * 1024 * 1024
MASKED = -1e30
LAG = 2


def segment_starts(seg_ref, segments):
    seg = seg_ref[...]
    starts = []
    for k in range(segments):
        below = jnp.where(seg < k, 1.0, 0.0)
        starts.append(jnp.sum(jnp.sum(below, axis=1, keepdims=True), axis=0, keepdims=True))
    return starts


def tenant_mask(starts, adapter_ref, first, rows, width):
    pos = (first + lax.broadcasted_iota(jnp.int32, (rows, width), 0)).astype(jnp.float32)
    column = lax.broadcasted_iota(jnp.int32, (rows, width), 1)
    column = (column // ADAPTER_RANK) % ADAPTER_COUNT
    tenant = jnp.zeros((rows, width), jnp.int32) + adapter_ref[0]
    for k in range(1, len(starts)):
        tenant = jnp.where(pos >= starts[k], adapter_ref[k], tenant)
    return column == tenant


def block_kernel(
    H, B, C, D, segments,
    x_ref, gain_ref, down_ref, wq_ref, wk_ref, wv_ref, uq_ref, uk_ref, uv_ref,
    wo_ref, out_down_ref, out_up_ref, seg_ref, key_pos_ref, adapter_ref,
    out_ref,
    rows_buf, weights, down, q_buf, kv, peak, total, left, out_weights, sent, landed,
    w_sem, o_sem, send_sem, recv_sem, kv_send, kv_recv, hop_send, hop_recv,
):
    u = lax.axis_index("uly")
    b = lax.axis_index("blk")
    rows, features = x_ref.shape
    part = rows // C
    kw = wk_ref.shape[1]
    qw = wq_ref.shape[1]
    width = features // D

    def weight_copies():
        return [
            pltpu.make_async_copy(down_ref, down, w_sem.at[0]),
            pltpu.make_async_copy(wk_ref, weights.at[:, pl.ds(0, kw)], w_sem.at[1]),
            pltpu.make_async_copy(wv_ref, weights.at[:, pl.ds(kw, kw)], w_sem.at[2]),
            pltpu.make_async_copy(wq_ref, weights.at[:, pl.ds(2 * kw, qw)], w_sem.at[3]),
        ]

    def output_copies():
        return [
            pltpu.make_async_copy(wo_ref, out_weights.at[pl.ds(0, qw), :], o_sem.at[0]),
            pltpu.make_async_copy(
                out_up_ref, out_weights.at[pl.ds(qw, HIDDEN), :], o_sem.at[1]
            ),
            pltpu.make_async_copy(
                out_up_ref, out_weights.at[pl.ds(qw + HIDDEN, HIDDEN), :], o_sem.at[2]
            ),
        ]

    for copy in weight_copies():
        copy.start()
    kv[...] = jnp.zeros_like(kv)

    barrier = pltpu.get_barrier_semaphore()

    @pl.when(u > 0)
    def _():
        pl.semaphore_signal(barrier, inc=1, device_id=(b, u - 1), device_id_type=MESH)

    @pl.when(u < H - 1)
    def _():
        pl.semaphore_signal(barrier, inc=1, device_id=(b, u + 1), device_id_type=MESH)

    chips = B // 2
    chip = b // 2
    core = b % 2
    sibling = b + 1 - 2 * core
    pl.semaphore_signal(barrier, inc=1, device_id=(sibling, u), device_id_type=MESH)
    for m in range(1, chips):
        pl.semaphore_signal(
            barrier, inc=1, device_id=(lax.rem(b + 2 * m, B), u), device_id_type=MESH
        )

    def send(j, c, side):
        where = rows_buf.at[j, pl.ds(c * part, part), :]
        return pltpu.make_async_remote_copy(
            src_ref=where,
            dst_ref=where,
            send_sem=send_sem.at[side, j, c],
            recv_sem=recv_sem.at[j, c],
            device_id=(b, u - 1 if side == 0 else u + 1),
            device_id_type=MESH,
        )

    def send_if(j, c):
        @pl.when((j >= u) & (u > 0))
        def _():
            send(j, c, 0).start()

        @pl.when((j <= u) & (u < H - 1))
        def _():
            send(j, c, 1).start()

    def normalize(c):
        values = x_ref[pl.ds(c * part, part), :].astype(jnp.float32)
        power = jnp.mean(values * values, axis=1, keepdims=True)
        normed = values * lax.rsqrt(power + eps_norm) * gain_ref[...]
        rows_buf[u, pl.ds(c * part, part), :] = normed.astype(jnp.bfloat16)

    normalize(0)

    @pl.when((u > 0) & (u < H - 1))
    def _():
        pl.semaphore_wait(barrier, chips + 2)

    @pl.when((u == 0) | (u == H - 1))
    def _():
        pl.semaphore_wait(barrier, chips + 1)

    send_if(u, 0)
    for c in range(1, C):
        normalize(c)
        send_if(u, c)

    starts = segment_starts(seg_ref, segments)
    for copy in weight_copies():
        copy.wait()
    for copy in output_copies():
        copy.start()

    def shard_rows(j):
        return pl.ds(pl.multiple_of(j * rows, rows), rows)

    def key_rows(block, j):
        return pl.ds(pl.multiple_of((j * B + block) * rows, rows), rows)

    def key_copy(block, j, sems, m, target):
        where = kv.at[key_rows(block, j), :]
        return pltpu.make_async_remote_copy(
            src_ref=where,
            dst_ref=where,
            send_sem=kv_send.at[sems, m, j],
            recv_sem=kv_recv.at[sems, m, j],
            device_id=(target, u),
            device_id_type=MESH,
        )

    def far(j, m):
        return key_copy(b, j, 0, m, b + 2 * m)

    def near(j):
        return key_copy(b, j, 0, 0, sibling)

    def passed(j, m):
        return key_copy(b - 2 * m, j, 1, m, sibling)

    def relay(d):
        def relay_side(side, carry):
            j = u + d * (1 - 2 * side)
            for m in range(1, chips):
                @pl.when((j >= 0) & (j < H) & (d + 1 > side) & (chip - m >= 0))
                def _():
                    far(j, m).wait_recv()
                    passed(j, m).start()

            return carry

        lax.fori_loop(0, jnp.where(d > 0, 2, 1), relay_side, 0)

    def project(j):
        shard = rows_buf[j]
        mask = tenant_mask(starts, adapter_ref, (b * H + j) * rows, rows, HIDDEN)

        def lowered(which):
            raw = jnp.dot(
                shard,
                down[:, which * HIDDEN : (which + 1) * HIDDEN],
                preferred_element_type=jnp.float32,
            )
            return jnp.where(mask, raw, 0.0).astype(jnp.bfloat16)

        def product(column, width, low, up):
            return (
                jnp.dot(
                    shard, weights[:, pl.ds(column, width)], preferred_element_type=jnp.float32
                )
                + adapter_scale * jnp.dot(low, up, preferred_element_type=jnp.float32)
            ).astype(jnp.bfloat16)

        kv[key_rows(b, j), :kw] = product(0, kw, lowered(1), uk_ref[...])
        kv[key_rows(b, j), kw:] = product(kw, kw, lowered(2), uv_ref[...])
        for m in range(1, chips):
            @pl.when(chip + m < chips)
            def _():
                far(j, m).start()

        @pl.when(core == 0)
        def _():
            near(j).start()

        low = lowered(0)
        step = 256

        def query_tile(n, carry):
            at = pl.multiple_of(n * step, step)
            q_buf[shard_rows(j), pl.ds(at, step)] = product(
                2 * kw + at, step, low, uq_ref[:, pl.ds(at, step)]
            )
            return carry

        lax.fori_loop(0, qw // step, query_tile, 0)

    at_end = (u == 0) | (u == H - 1)

    def await_keys(known):
        def keys_arrived(j, carry):
            early = at_end & (j != H - 1 - u)
            due = early if known else jnp.logical_not(early)
            for m in range(1, chips):
                @pl.when((chip - m >= 0) & due)
                def _():
                    passed(j, m).wait_recv()

            @pl.when((core == 1) & due)
            def _():
                near(j).wait_recv()

            return carry

        lax.fori_loop(0, H, keys_arrived, 0)

    groups = kw // HEAD_SIZE
    group = QUERY_HEADS // KEY_VALUE_HEADS
    scale = math.log2(math.e) / math.sqrt(HEAD_SIZE)

    T = B * rows
    first_left = jnp.where(u > 1, 1, 0)
    first_right = jnp.where(u < H - 2, H - 2, H - 1)

    def clear():
        peak[...] = jnp.full_like(peak, MASKED)
        total[...] = jnp.zeros_like(total)

    def visit(j, needed):
        at_rows = shard_rows(j)
        first = (b * H + j) * rows
        pos = (first + lax.broadcasted_iota(jnp.int32, (rows, 1), 0)).astype(jnp.float32)
        lower = jnp.zeros((rows, 1), jnp.float32)
        for k in range(1, segments):
            lower = jnp.where(pos >= starts[k], starts[k], lower)

        def key_tile(index):
            at_keys = pl.ds(pl.multiple_of(index * T, T), T)
            key_pos = key_pos_ref[...] + (index * rows).astype(jnp.float32)
            bias = jnp.where((key_pos <= pos) & (key_pos >= lower), 0.0, MASKED)
            for g in range(groups):
                keys = kv[at_keys, g * HEAD_SIZE : (g + 1) * HEAD_SIZE]
                values = kv[at_keys, (groups + g) * HEAD_SIZE : (groups + g + 1) * HEAD_SIZE]
                values = jnp.concatenate([values, jnp.ones_like(values)], axis=1)
                query = jnp.concatenate(
                    [
                        q_buf[at_rows, h * HEAD_SIZE : (h + 1) * HEAD_SIZE]
                        for h in range(g * group, (g + 1) * group)
                    ],
                    axis=0,
                )
                scores = lax.dot_general(
                    query, keys, (((1,), (1,)), ((), ())), preferred_element_type=jnp.float32
                )
                scores = scores.reshape(group, rows, T) * scale + bias[None]
                scores = scores.reshape(group * rows, T)
                before = peak[g]
                fresh = jnp.maximum(before, jnp.max(scores, axis=1, keepdims=True))
                shares = jnp.exp2(scores - fresh[:, :1]).astype(jnp.bfloat16)
                decay = jnp.exp2(before - fresh)
                peak[g] = fresh
                total[g] = total[g] * jnp.concatenate([decay, decay], axis=1) + jnp.dot(
                    shares, values, preferred_element_type=jnp.float32
                )

        def maybe(index, inner):
            @pl.when(needed(index))
            def _():
                key_tile(index)

            return inner

        lax.fori_loop(0, H, maybe, 0)

    def conclude(j):
        at_rows = shard_rows(j)
        first = (b * H + j) * rows
        for h in range(groups * group):
            g, at = h // group, (h % group) * rows
            left[at_rows, h * HEAD_SIZE : (h + 1) * HEAD_SIZE] = (
                total[g, at : at + rows, :HEAD_SIZE] / total[g, at : at + rows, HEAD_SIZE:]
            ).astype(jnp.bfloat16)
        lows = jnp.dot(
            left[at_rows, :qw], out_down_ref[...], preferred_element_type=jnp.float32
        )
        mask = tenant_mask(starts, adapter_ref, first, rows, HIDDEN)
        lows = jnp.where(mask, adapter_scale * lows, 0.0)
        high = lows.astype(jnp.bfloat16)
        left[at_rows, qw : qw + HIDDEN] = high
        left[at_rows, qw + HIDDEN :] = (lows - high.astype(jnp.float32)).astype(jnp.bfloat16)

    def phase(d, carry):
        @pl.when((d > 0) & at_end)
        def _():
            relay(d - 1)

        @pl.when((d == H - 1) & at_end)
        def _():
            await_keys(True)
            clear()
            visit(jnp.where(u == 0, first_right, first_left), lambda s: s != H - 1 - u)

        @pl.when(d > 0)
        def _():
            for c in range(C):
                @pl.when(u + d < H)
                def _():
                    send(u + d, c, 0).wait_recv()

                    @pl.when(u > 0)
                    def _():
                        send(u + d, c, 0).start()

                @pl.when(u - d >= 0)
                def _():
                    send(u - d, c, 1).wait_recv()

                    @pl.when(u < H - 1)
                    def _():
                        send(u - d, c, 1).start()

        @pl.when((d > 0) & jnp.logical_not(at_end))
        def _():
            relay(d - 1)

        def side_step(side, inner):
            j = u + d * (1 - 2 * side)

            @pl.when((j >= 0) & (j < H) & (d + 1 > side))
            def _():
                project(j)

            return inner

        lax.fori_loop(0, jnp.where(d > 0, 2, 1), side_step, 0)
        return carry

    lax.fori_loop(0, H, phase, 0)

    relay(H - 1)
    await_keys(False)

    def own_part(j, c):
        columns = pl.ds(pl.multiple_of(c * width, width), width)
        return jnp.dot(
            left[shard_rows(j), :], out_weights[:, columns], preferred_element_type=jnp.float32
        )

    def hop(j, c, side):
        return pltpu.make_async_remote_copy(
            src_ref=sent.at[j, c],
            dst_ref=landed.at[side, j, c],
            send_sem=hop_send.at[j, c],
            recv_sem=hop_recv.at[side, j, c],
            device_id=(b, u + 2 * side - 1),
            device_id_type=MESH,
        )

    for copy in output_copies():
        copy.wait()

    hops = (H - 1) * D
    final = 1 + hops + LAG * (H - 2)

    def place(n, side):
        p = n // D
        p = jnp.where(p < 2, 1 - p, p)
        j = jnp.where(side == 0, p, H - 1 - p)
        sends = jnp.where(side == 0, u - j, j - u) > 0
        return j, n % D, sends

    def step(t, carry):
        def position(side):
            behind = jnp.where(side == 0, H - 1 - u, u)
            n = t - 1 - LAG * jnp.maximum(behind - 1, 0)
            return jnp.clip(n, 0, hops - 1), (n >= 0) & (n < hops), behind

        def attend_side(side, side_carry):
            n, inside, _ = position(side)
            j, c, sends = place(n, side)
            started = jnp.where(side == 0, first_left, first_right)
            opens = jnp.where(side == 0, u, H - 1 - u) > 0
            due = inside & (c == 0) & sends & (j != started)

            @pl.when(((t == 0) & opens) | ((t < final) & due) | ((t == final) & (side == 0)))
            def _():
                shard = jnp.where(t == 0, started, jnp.where(t == final, u, j))
                resumed = (t == 0) & at_end

                @pl.when(jnp.logical_not(resumed))
                def _():
                    clear()

                visit(shard, lambda s: (s == H - 1 - u) | jnp.logical_not(resumed))
                conclude(shard)

            return side_carry

        lax.fori_loop(0, 2, attend_side, 0)

        def pass_on(side, side_carry):
            n, inside, behind = position(side)
            j, c, sends = place(n, side)

            @pl.when(inside & sends)
            def _():
                value = own_part(j, c)

                @pl.when(behind > 0)
                def _():
                    hop(j, c, side).wait_recv()
                    sent[j, c] = (value + landed[side, j, c].astype(jnp.float32)).astype(
                        jnp.bfloat16
                    )

                @pl.when(behind == 0)
                def _():
                    sent[j, c] = value.astype(jnp.bfloat16)

                hop(j, c, side).start()

            return side_carry

        lax.fori_loop(0, 2, pass_on, 0)
        return carry

    lax.fori_loop(0, final + 1, step, 0)

    def last(c, carry):
        columns = pl.ds(pl.multiple_of(c * width, width), width)
        value = own_part(u, c)

        @pl.when(u > 0)
        def _():
            hop(u, c, 1).wait_recv()

        @pl.when(u < H - 1)
        def _():
            hop(u, c, 0).wait_recv()

        from_left = jnp.where(u > 0, landed[1, u, c].astype(jnp.float32), 0.0)
        from_right = jnp.where(u < H - 1, landed[0, u, c].astype(jnp.float32), 0.0)
        out_ref[:, columns] = (value + from_left + from_right).astype(jnp.bfloat16)
        return carry

    lax.fori_loop(0, D, last, 0)

    def finish(j, carry):
        for c in range(C):
            @pl.when((j >= u) & (u > 0))
            def _():
                send(j, c, 0).wait_send()

            @pl.when((j <= u) & (u < H - 1))
            def _():
                send(j, c, 1).wait_send()

        for m in range(1, chips):
            @pl.when(chip + m < chips)
            def _():
                far(j, m).wait_send()

            @pl.when(chip - m >= 0)
            def _():
                passed(j, m).wait_send()

        @pl.when(core == 0)
        def _():
            near(j).wait_send()

        for c in range(D):
            @pl.when(j != u)
            def _():
                hop(j, c, jnp.where(j < u, 0, 1)).wait_send()

        return carry

    lax.fori_loop(0, H, finish, 0)


IN_VMEM = pl.BlockSpec(memory_space=pltpu.VMEM)
IN_SMEM = pl.BlockSpec(memory_space=pltpu.SMEM)
ANYWHERE = pl.BlockSpec(memory_space=pl.ANY)


def shards(
    activations,
    input_norm_gain,
    query_weight,
    key_weight,
    value_weight,
    output_weight,
    adapter_down_maps,
    query_up_maps,
    key_up_maps,
    value_up_maps,
    output_down_maps,
    output_up_maps,
    segment_index,
    segment_adapter,
):
    H = lax.axis_size("uly")
    B = lax.axis_size("blk")
    rows, features = activations.shape
    tokens = segment_index.shape[0]
    segments = segment_adapter.shape[0]
    qw = query_weight.shape[1]
    kw = key_weight.shape[1]
    block_rows = rows * H
    seg = segment_index.reshape(tokens // 128, 128)
    bf16 = jnp.bfloat16
    C, D = 3, 4
    key_pos = np.arange(B)[:, None] * block_rows + np.arange(rows)[None, :]
    key_pos = jnp.asarray(key_pos.reshape(1, B * rows), jnp.float32)
    group_rows = QUERY_HEADS // KEY_VALUE_HEADS * rows
    groups = kw // HEAD_SIZE
    f32 = jnp.float32
    return pl.pallas_call(
        functools.partial(block_kernel, H, B, C, D, segments),
        out_shape=jax.ShapeDtypeStruct((rows, features), bf16),
        in_specs=[IN_VMEM] * 2
        + [ANYWHERE] * 4
        + [IN_VMEM] * 3
        + [ANYWHERE, IN_VMEM, ANYWHERE, IN_VMEM, IN_VMEM, IN_SMEM],
        out_specs=IN_VMEM,
        scratch_shapes=[
            pltpu.VMEM((H, rows, features), bf16),
            pltpu.VMEM((features, qw + 2 * kw), bf16),
            pltpu.VMEM(adapter_down_maps.shape, bf16),
            pltpu.VMEM((block_rows, qw), bf16),
            pltpu.VMEM((tokens, 2 * kw), bf16),
            pltpu.VMEM((groups, group_rows, HEAD_SIZE), f32),
            pltpu.VMEM((groups, group_rows, 2 * HEAD_SIZE), f32),
            pltpu.VMEM((block_rows, qw + 2 * HIDDEN), bf16),
            pltpu.VMEM((qw + 2 * HIDDEN, features), bf16),
            pltpu.VMEM((H, D, rows, features // D), bf16),
            pltpu.VMEM((2, H, D, rows, features // D), bf16),
            pltpu.SemaphoreType.DMA((4,)),
            pltpu.SemaphoreType.DMA((3,)),
            pltpu.SemaphoreType.DMA((2, H, C)),
            pltpu.SemaphoreType.DMA((H, C)),
            pltpu.SemaphoreType.DMA((2, B // 2, H)),
            pltpu.SemaphoreType.DMA((2, B // 2, H)),
            pltpu.SemaphoreType.DMA((H, D)),
            pltpu.SemaphoreType.DMA((2, H, D)),
        ],
        compiler_params=pltpu.CompilerParams(
            collective_id=0, has_side_effects=True, vmem_limit_bytes=VMEM_LIMIT
        ),
        name="attention_block",
    )(
        activations,
        input_norm_gain.reshape(1, features),
        adapter_down_maps,
        query_weight,
        key_weight,
        value_weight,
        query_up_maps,
        key_up_maps,
        value_up_maps,
        output_weight,
        output_down_maps,
        output_up_maps,
        seg,
        key_pos,
        segment_adapter,
    )


def solution(mesh):
    return jax.shard_map(
        shards,
        mesh=mesh,
        in_specs=(
            P(("blk", "uly"), None),
            P(),
            P(None, "uly"),
            P(None, "uly"),
            P(None, "uly"),
            P("uly", None),
            P(),
            P(None, "uly"),
            P(None, "uly"),
            P(None, "uly"),
            P("uly", None),
            P(),
            P(),
            P(),
        ),
        out_specs=P(("blk", "uly"), None),
        check_vma=False,
    )
```

```python
import functools
import math

import jax
import jax.numpy as jnp
import numpy as np
from jax import lax
from jax.experimental import pallas as pl
from jax.experimental.pallas import tpu as pltpu
from jax.sharding import PartitionSpec as P

QUERY_HEADS = 32
KEY_VALUE_HEADS = 8
HEAD_SIZE = 128
ADAPTER_RANK = 16
ADAPTER_COUNT = 8
HIDDEN = ADAPTER_COUNT * ADAPTER_RANK

eps_norm = 1e-05
adapter_scale = 2.0
MESH = pl.DeviceIdType.MESH
VMEM_LIMIT = 60 * 1024 * 1024
MASKED = -1e30
LAG = 4


def segment_starts(seg_ref, segments):
    seg = seg_ref[...]
    starts = []
    for k in range(segments):
        below = jnp.where(seg < k, 1.0, 0.0)
        starts.append(jnp.sum(jnp.sum(below, axis=1, keepdims=True), axis=0, keepdims=True))
    return starts


def tenant_mask(starts, adapter_ref, first, rows, width):
    pos = (first + lax.broadcasted_iota(jnp.int32, (rows, width), 0)).astype(jnp.float32)
    column = lax.broadcasted_iota(jnp.int32, (rows, width), 1)
    column = (column // ADAPTER_RANK) % ADAPTER_COUNT
    tenant = jnp.zeros((rows, width), jnp.int32) + adapter_ref[0]
    for k in range(1, len(starts)):
        tenant = jnp.where(pos >= starts[k], adapter_ref[k], tenant)
    return column == tenant


def block_kernel(
    H, B, C, D, segments,
    x_ref, gain_ref, down_ref, wq_ref, wk_ref, wv_ref, uq_ref, uk_ref, uv_ref,
    wo_ref, out_down_ref, out_up_ref, seg_ref, key_pos_ref, adapter_ref,
    out_ref,
    rows_buf, weights, down, q_buf, kv, peak, total, left, out_weights, sent, landed,
    w_sem, o_sem, send_sem, recv_sem, kv_send, kv_recv, hop_send, hop_recv,
):
    u = lax.axis_index("uly")
    b = lax.axis_index("blk")
    rows, features = x_ref.shape
    part = rows // C
    kw = wk_ref.shape[1]
    qw = wq_ref.shape[1]
    width = features // D

    def weight_copies():
        return [
            pltpu.make_async_copy(down_ref, down, w_sem.at[0]),
            pltpu.make_async_copy(wk_ref, weights.at[:, pl.ds(0, kw)], w_sem.at[1]),
            pltpu.make_async_copy(wv_ref, weights.at[:, pl.ds(kw, kw)], w_sem.at[2]),
            pltpu.make_async_copy(wq_ref, weights.at[:, pl.ds(2 * kw, qw)], w_sem.at[3]),
        ]

    def output_copies():
        return [
            pltpu.make_async_copy(wo_ref, out_weights.at[pl.ds(0, qw), :], o_sem.at[0]),
            pltpu.make_async_copy(
                out_up_ref, out_weights.at[pl.ds(qw, HIDDEN), :], o_sem.at[1]
            ),
            pltpu.make_async_copy(
                out_up_ref, out_weights.at[pl.ds(qw + HIDDEN, HIDDEN), :], o_sem.at[2]
            ),
        ]

    for copy in weight_copies():
        copy.start()
    kv[...] = jnp.zeros_like(kv)

    barrier = pltpu.get_barrier_semaphore()

    @pl.when(u > 0)
    def _():
        pl.semaphore_signal(barrier, inc=1, device_id=(b, u - 1), device_id_type=MESH)

    @pl.when(u < H - 1)
    def _():
        pl.semaphore_signal(barrier, inc=1, device_id=(b, u + 1), device_id_type=MESH)

    chips = B // 2
    chip = b // 2
    core = b % 2
    sibling = b + 1 - 2 * core
    pl.semaphore_signal(barrier, inc=1, device_id=(sibling, u), device_id_type=MESH)
    for m in range(1, chips):
        pl.semaphore_signal(
            barrier, inc=1, device_id=(lax.rem(b + 2 * m, B), u), device_id_type=MESH
        )

    def send(j, c, side):
        where = rows_buf.at[j, pl.ds(c * part, part), :]
        return pltpu.make_async_remote_copy(
            src_ref=where,
            dst_ref=where,
            send_sem=send_sem.at[side, j, c],
            recv_sem=recv_sem.at[j, c],
            device_id=(b, u - 1 if side == 0 else u + 1),
            device_id_type=MESH,
        )

    def send_if(j, c):
        @pl.when((j >= u) & (u > 0))
        def _():
            send(j, c, 0).start()

        @pl.when((j <= u) & (u < H - 1))
        def _():
            send(j, c, 1).start()

    def normalize(c):
        values = x_ref[pl.ds(c * part, part), :].astype(jnp.float32)
        power = jnp.mean(values * values, axis=1, keepdims=True)
        normed = values * lax.rsqrt(power + eps_norm) * gain_ref[...]
        rows_buf[u, pl.ds(c * part, part), :] = normed.astype(jnp.bfloat16)

    normalize(0)

    @pl.when((u > 0) & (u < H - 1))
    def _():
        pl.semaphore_wait(barrier, chips + 2)

    @pl.when((u == 0) | (u == H - 1))
    def _():
        pl.semaphore_wait(barrier, chips + 1)

    send_if(u, 0)
    for c in range(1, C):
        normalize(c)
        send_if(u, c)

    starts = segment_starts(seg_ref, segments)
    for copy in weight_copies():
        copy.wait()
    for copy in output_copies():
        copy.start()

    def shard_rows(j):
        return pl.ds(pl.multiple_of(j * rows, rows), rows)

    def key_rows(block, j):
        return pl.ds(pl.multiple_of((j * B + block) * rows, rows), rows)

    def key_copy(block, j, sems, m, target):
        where = kv.at[key_rows(block, j), :]
        return pltpu.make_async_remote_copy(
            src_ref=where,
            dst_ref=where,
            send_sem=kv_send.at[sems, m, j],
            recv_sem=kv_recv.at[sems, m, j],
            device_id=(target, u),
            device_id_type=MESH,
        )

    def far(j, m):
        return key_copy(b, j, 0, m, b + 2 * m)

    def near(j):
        return key_copy(b, j, 0, 0, sibling)

    def passed(j, m):
        return key_copy(b - 2 * m, j, 1, m, sibling)

    def relay(d):
        def relay_side(side, carry):
            j = u + d * (1 - 2 * side)
            for m in range(1, chips):
                @pl.when((j >= 0) & (j < H) & (d + 1 > side) & (chip - m >= 0))
                def _():
                    far(j, m).wait_recv()
                    passed(j, m).start()

            return carry

        lax.fori_loop(0, jnp.where(d > 0, 2, 1), relay_side, 0)

    def project(j):
        shard = rows_buf[j]
        mask = tenant_mask(starts, adapter_ref, (b * H + j) * rows, rows, HIDDEN)

        def lowered(which):
            raw = jnp.dot(
                shard,
                down[:, which * HIDDEN : (which + 1) * HIDDEN],
                preferred_element_type=jnp.float32,
            )
            return jnp.where(mask, raw, 0.0).astype(jnp.bfloat16)

        def product(column, width, low, up):
            return (
                jnp.dot(
                    shard, weights[:, pl.ds(column, width)], preferred_element_type=jnp.float32
                )
                + adapter_scale * jnp.dot(low, up, preferred_element_type=jnp.float32)
            ).astype(jnp.bfloat16)

        kv[key_rows(b, j), :kw] = product(0, kw, lowered(1), uk_ref[...])
        kv[key_rows(b, j), kw:] = product(kw, kw, lowered(2), uv_ref[...])
        for m in range(1, chips):
            @pl.when(chip + m < chips)
            def _():
                far(j, m).start()

        @pl.when(core == 0)
        def _():
            near(j).start()

        low = lowered(0)
        step = 256

        def query_tile(n, carry):
            at = pl.multiple_of(n * step, step)
            q_buf[shard_rows(j), pl.ds(at, step)] = product(
                2 * kw + at, step, low, uq_ref[:, pl.ds(at, step)]
            )
            return carry

        lax.fori_loop(0, qw // step, query_tile, 0)

    at_end = (u == 0) | (u == H - 1)

    def await_keys(known):
        def keys_arrived(j, carry):
            early = at_end & (j != H - 1 - u)
            due = early if known else jnp.logical_not(early)
            for m in range(1, chips):
                @pl.when((chip - m >= 0) & due)
                def _():
                    passed(j, m).wait_recv()

            @pl.when((core == 1) & due)
            def _():
                near(j).wait_recv()

            return carry

        lax.fori_loop(0, H, keys_arrived, 0)

    groups = kw // HEAD_SIZE
    group = QUERY_HEADS // KEY_VALUE_HEADS
    scale = math.log2(math.e) / math.sqrt(HEAD_SIZE)

    T = B * rows
    first_left = jnp.where(u > 1, 1, 0)
    first_right = jnp.where(u < H - 2, H - 2, H - 1)

    def clear():
        peak[...] = jnp.full_like(peak, MASKED)
        total[...] = jnp.zeros_like(total)

    def visit(j, needed):
        at_rows = shard_rows(j)
        first = (b * H + j) * rows
        pos = (first + lax.broadcasted_iota(jnp.int32, (rows, 1), 0)).astype(jnp.float32)
        lower = jnp.zeros((rows, 1), jnp.float32)
        for k in range(1, segments):
            lower = jnp.where(pos >= starts[k], starts[k], lower)

        def key_tile(index):
            at_keys = pl.ds(pl.multiple_of(index * T, T), T)
            key_pos = key_pos_ref[...] + (index * rows).astype(jnp.float32)
            bias = jnp.where((key_pos <= pos) & (key_pos >= lower), 0.0, MASKED)
            for g in range(groups):
                keys = kv[at_keys, g * HEAD_SIZE : (g + 1) * HEAD_SIZE]
                values = kv[at_keys, (groups + g) * HEAD_SIZE : (groups + g + 1) * HEAD_SIZE]
                values = jnp.concatenate([values, jnp.ones_like(values)], axis=1)
                query = jnp.concatenate(
                    [
                        q_buf[at_rows, h * HEAD_SIZE : (h + 1) * HEAD_SIZE]
                        for h in range(g * group, (g + 1) * group)
                    ],
                    axis=0,
                )
                scores = lax.dot_general(
                    query, keys, (((1,), (1,)), ((), ())), preferred_element_type=jnp.float32
                )
                scores = scores.reshape(group, rows, T) * scale + bias[None]
                scores = scores.reshape(group * rows, T)
                before = peak[g]
                fresh = jnp.maximum(before, jnp.max(scores, axis=1, keepdims=True))
                shares = jnp.exp2(scores - fresh[:, :1]).astype(jnp.bfloat16)
                decay = jnp.exp2(before - fresh)
                peak[g] = fresh
                total[g] = total[g] * jnp.concatenate([decay, decay], axis=1) + jnp.dot(
                    shares, values, preferred_element_type=jnp.float32
                )

        def maybe(index, inner):
            @pl.when(needed(index))
            def _():
                key_tile(index)

            return inner

        lax.fori_loop(0, H, maybe, 0)

    def conclude(j):
        at_rows = shard_rows(j)
        first = (b * H + j) * rows
        for h in range(groups * group):
            g, at = h // group, (h % group) * rows
            left[at_rows, h * HEAD_SIZE : (h + 1) * HEAD_SIZE] = (
                total[g, at : at + rows, :HEAD_SIZE] / total[g, at : at + rows, HEAD_SIZE:]
            ).astype(jnp.bfloat16)
        lows = jnp.dot(
            left[at_rows, :qw], out_down_ref[...], preferred_element_type=jnp.float32
        )
        mask = tenant_mask(starts, adapter_ref, first, rows, HIDDEN)
        lows = jnp.where(mask, adapter_scale * lows, 0.0)
        high = lows.astype(jnp.bfloat16)
        left[at_rows, qw : qw + HIDDEN] = high
        left[at_rows, qw + HIDDEN :] = (lows - high.astype(jnp.float32)).astype(jnp.bfloat16)

    def phase(d, carry):
        @pl.when((d > 0) & at_end)
        def _():
            relay(d - 1)

        @pl.when((d == H - 1) & at_end)
        def _():
            await_keys(True)
            clear()
            visit(jnp.where(u == 0, first_right, first_left), lambda s: s != H - 1 - u)

        @pl.when(d > 0)
        def _():
            for c in range(C):
                @pl.when(u + d < H)
                def _():
                    send(u + d, c, 0).wait_recv()

                    @pl.when(u > 0)
                    def _():
                        send(u + d, c, 0).start()

                @pl.when(u - d >= 0)
                def _():
                    send(u - d, c, 1).wait_recv()

                    @pl.when(u < H - 1)
                    def _():
                        send(u - d, c, 1).start()

        @pl.when((d > 0) & jnp.logical_not(at_end))
        def _():
            relay(d - 1)

        def side_step(side, inner):
            j = u + d * (1 - 2 * side)

            @pl.when((j >= 0) & (j < H) & (d + 1 > side))
            def _():
                project(j)

            return inner

        lax.fori_loop(0, jnp.where(d > 0, 2, 1), side_step, 0)
        return carry

    lax.fori_loop(0, H, phase, 0)

    relay(H - 1)
    await_keys(False)

    def own_part(j, c):
        columns = pl.ds(pl.multiple_of(c * width, width), width)
        return jnp.dot(
            left[shard_rows(j), :], out_weights[:, columns], preferred_element_type=jnp.float32
        )

    def hop(j, c, side):
        return pltpu.make_async_remote_copy(
            src_ref=sent.at[j, c],
            dst_ref=landed.at[side, j, c],
            send_sem=hop_send.at[j, c],
            recv_sem=hop_recv.at[side, j, c],
            device_id=(b, u + 2 * side - 1),
            device_id_type=MESH,
        )

    for copy in output_copies():
        copy.wait()

    hops = (H - 1) * D
    final = 1 + hops + LAG * (H - 2)

    def place(n, side):
        p = n // D
        p = jnp.where(p < 2, 1 - p, p)
        j = jnp.where(side == 0, p, H - 1 - p)
        sends = jnp.where(side == 0, u - j, j - u) > 0
        return j, n % D, sends

    def step(t, carry):
        def position(side):
            behind = jnp.where(side == 0, H - 1 - u, u)
            n = t - 1 - LAG * jnp.maximum(behind - 1, 0)
            return jnp.clip(n, 0, hops - 1), (n >= 0) & (n < hops), behind

        def attend_side(side, side_carry):
            n, inside, _ = position(side)
            j, c, sends = place(n, side)
            started = jnp.where(side == 0, first_left, first_right)
            opens = jnp.where(side == 0, u, H - 1 - u) > 0
            due = inside & (c == 0) & sends & (j != started)

            @pl.when(((t == 0) & opens) | ((t < final) & due) | ((t == final) & (side == 0)))
            def _():
                shard = jnp.where(t == 0, started, jnp.where(t == final, u, j))
                resumed = (t == 0) & at_end

                @pl.when(jnp.logical_not(resumed))
                def _():
                    clear()

                visit(shard, lambda s: (s == H - 1 - u) | jnp.logical_not(resumed))
                conclude(shard)

            return side_carry

        lax.fori_loop(0, 2, attend_side, 0)

        def pass_on(side, side_carry):
            n, inside, behind = position(side)
            j, c, sends = place(n, side)

            @pl.when(inside & sends)
            def _():
                value = own_part(j, c)

                @pl.when(behind > 0)
                def _():
                    hop(j, c, side).wait_recv()
                    sent[j, c] = (value + landed[side, j, c].astype(jnp.float32)).astype(
                        jnp.bfloat16
                    )

                @pl.when(behind == 0)
                def _():
                    sent[j, c] = value.astype(jnp.bfloat16)

                hop(j, c, side).start()

            return side_carry

        lax.fori_loop(0, 2, pass_on, 0)
        return carry

    lax.fori_loop(0, final + 1, step, 0)

    def last(c, carry):
        columns = pl.ds(pl.multiple_of(c * width, width), width)
        value = own_part(u, c)

        @pl.when(u > 0)
        def _():
            hop(u, c, 1).wait_recv()

        @pl.when(u < H - 1)
        def _():
            hop(u, c, 0).wait_recv()

        from_left = jnp.where(u > 0, landed[1, u, c].astype(jnp.float32), 0.0)
        from_right = jnp.where(u < H - 1, landed[0, u, c].astype(jnp.float32), 0.0)
        out_ref[:, columns] = (value + from_left + from_right).astype(jnp.bfloat16)
        return carry

    lax.fori_loop(0, D, last, 0)

    def finish(j, carry):
        for c in range(C):
            @pl.when((j >= u) & (u > 0))
            def _():
                send(j, c, 0).wait_send()

            @pl.when((j <= u) & (u < H - 1))
            def _():
                send(j, c, 1).wait_send()

        for m in range(1, chips):
            @pl.when(chip + m < chips)
            def _():
                far(j, m).wait_send()

            @pl.when(chip - m >= 0)
            def _():
                passed(j, m).wait_send()

        @pl.when(core == 0)
        def _():
            near(j).wait_send()

        for c in range(D):
            @pl.when(j != u)
            def _():
                hop(j, c, jnp.where(j < u, 0, 1)).wait_send()

        return carry

    lax.fori_loop(0, H, finish, 0)


IN_VMEM = pl.BlockSpec(memory_space=pltpu.VMEM)
IN_SMEM = pl.BlockSpec(memory_space=pltpu.SMEM)
ANYWHERE = pl.BlockSpec(memory_space=pl.ANY)


def shards(
    activations,
    input_norm_gain,
    query_weight,
    key_weight,
    value_weight,
    output_weight,
    adapter_down_maps,
    query_up_maps,
    key_up_maps,
    value_up_maps,
    output_down_maps,
    output_up_maps,
    segment_index,
    segment_adapter,
):
    H = lax.axis_size("uly")
    B = lax.axis_size("blk")
    rows, features = activations.shape
    tokens = segment_index.shape[0]
    segments = segment_adapter.shape[0]
    qw = query_weight.shape[1]
    kw = key_weight.shape[1]
    block_rows = rows * H
    seg = segment_index.reshape(tokens // 128, 128)
    bf16 = jnp.bfloat16
    C, D = 3, 8
    key_pos = np.arange(B)[:, None] * block_rows + np.arange(rows)[None, :]
    key_pos = jnp.asarray(key_pos.reshape(1, B * rows), jnp.float32)
    group_rows = QUERY_HEADS // KEY_VALUE_HEADS * rows
    groups = kw // HEAD_SIZE
    f32 = jnp.float32
    return pl.pallas_call(
        functools.partial(block_kernel, H, B, C, D, segments),
        out_shape=jax.ShapeDtypeStruct((rows, features), bf16),
        in_specs=[IN_VMEM] * 2
        + [ANYWHERE] * 4
        + [IN_VMEM] * 3
        + [ANYWHERE, IN_VMEM, ANYWHERE, IN_VMEM, IN_VMEM, IN_SMEM],
        out_specs=IN_VMEM,
        scratch_shapes=[
            pltpu.VMEM((H, rows, features), bf16),
            pltpu.VMEM((features, qw + 2 * kw), bf16),
            pltpu.VMEM(adapter_down_maps.shape, bf16),
            pltpu.VMEM((block_rows, qw), bf16),
            pltpu.VMEM((tokens, 2 * kw), bf16),
            pltpu.VMEM((groups, group_rows, HEAD_SIZE), f32),
            pltpu.VMEM((groups, group_rows, 2 * HEAD_SIZE), f32),
            pltpu.VMEM((block_rows, qw + 2 * HIDDEN), bf16),
            pltpu.VMEM((qw + 2 * HIDDEN, features), bf16),
            pltpu.VMEM((H, D, rows, features // D), bf16),
            pltpu.VMEM((2, H, D, rows, features // D), bf16),
            pltpu.SemaphoreType.DMA((4,)),
            pltpu.SemaphoreType.DMA((3,)),
            pltpu.SemaphoreType.DMA((2, H, C)),
            pltpu.SemaphoreType.DMA((H, C)),
            pltpu.SemaphoreType.DMA((2, B // 2, H)),
            pltpu.SemaphoreType.DMA((2, B // 2, H)),
            pltpu.SemaphoreType.DMA((H, D)),
            pltpu.SemaphoreType.DMA((2, H, D)),
        ],
        compiler_params=pltpu.CompilerParams(
            collective_id=0, has_side_effects=True, vmem_limit_bytes=VMEM_LIMIT
        ),
        name="attention_block",
    )(
        activations,
        input_norm_gain.reshape(1, features),
        adapter_down_maps,
        query_weight,
        key_weight,
        value_weight,
        query_up_maps,
        key_up_maps,
        value_up_maps,
        output_weight,
        output_down_maps,
        output_up_maps,
        seg,
        key_pos,
        segment_adapter,
    )


def solution(mesh):
    return jax.shard_map(
        shards,
        mesh=mesh,
        in_specs=(
            P(("blk", "uly"), None),
            P(),
            P(None, "uly"),
            P(None, "uly"),
            P(None, "uly"),
            P("uly", None),
            P(),
            P(None, "uly"),
            P(None, "uly"),
            P(None, "uly"),
            P("uly", None),
            P(),
            P(),
            P(),
        ),
        out_specs=P(("blk", "uly"), None),
        check_vma=False,
    )
```
